256 devices in a mesh: head: 16 (over z, x_lo), blk: 16 (over x_hi, y, core).
Axes of the slice: x: 4 (x_hi: 2, x_lo: 2; x = x_hi * 2 + x_lo), y: 4, z: 8, core: 2. Of those that a mesh axis runs over, the one named last changes fastest.
Arguments:
- qkv: bfloat16 [16, 2048, 6144], P('blk', 'head'), may hold values from -9 to 9
- query_blocks: int32 [64], P('blk'), may hold values from 0 to 255, as said below
- out_weight: bfloat16 [2048, 3072], P('head')
- mod_shift: float32 [3072], replicated, may hold values from -3 to 3
- mod_scale: float32 [3072], replicated, may hold values from -3 to 3
- final_weight: bfloat16 [3072, 64], replicated, may hold values from -0.109375 to 0.109375
- final_bias: float32 [64], replicated, may hold values from -3 to 3
- conv_in_weight: bfloat16 [3, 3, 3, 16, 512], replicated, may hold values from -0.3125 to 0.3125
- conv_in_bias: float32 [512], replicated, may hold values from -3 to 3
- conv_weight: bfloat16 [3, 3, 3, 512, 512], P(None, None, None, None, 'head'), may hold values from -0.0546875 to 0.0546875
- conv_bias: float32 [512], replicated, may hold values from -3 to 3
Outputs:
- vae_features: bfloat16 [8, 64, 64, 512], P(None, 'blk', 'head')
The draws below stay inside these ranges and needn't reach their ends.
Inputs may be any that keep to these rules, and one draw needn't show every extreme that they name: `query_blocks`: entry i names a block of 128 token rows among the 16 blocks held by index i // 4 of blk, that is from 16 * (i // 4) to 16 * (i // 4 + 1) - 1; the 4 entries of one index of blk are distinct, one from each run of 4 blocks, in any order.
All inputs are finite; a program needn't handle non-finite values.
Results may differ from the reference program's by a relative error of at most 0.023.
Values may be sent and summed in bfloat16 or wider, within the bound.
No kernel may reach another device: no remote copies, remote signals or barrier semaphores. Data moves between devices by JAX's collectives and lax.ppermute only.
A program may use at most 192 MiB of HBM per device.

```python
import math
import jax
import jax.numpy as jnp
from jax import lax

D = 3072
HEADS = 16
HD = 128
LAT = 16
CH = 512
QBLK = 128
TF = 8
TH = 2
TW = 2
S = 32768
BPS = 16
QB_DEV = 4
QPB = 512
LH = 64
LW = 64
PCH = 64
N_HEAD = 16
N_BLK = 16


def draw_qkv(key, part):
    key = jax.random.fold_in(key, 17)
    subkeys = jax.random.split(key, 1)
    shape = (S, 3, HEADS, HD)
    base = jax.random.normal(subkeys[0], shape, jnp.float32)
    factor = jnp.array([4.0, 1.0, 1.0], jnp.float32).reshape(1, 3, 1, 1)
    limit = jnp.array([9.0, 5.0, 5.0], jnp.float32).reshape(1, 3, 1, 1)
    stacked = jnp.clip(base * factor, -limit, limit)
    return stacked.reshape(S // (BPS * QBLK), BPS * QBLK, 3 * HEADS * HD).astype(jnp.bfloat16)


def draw_out_weight(key, part):
    key = jax.random.fold_in(key, 29)
    subkeys = jax.random.split(key, 1)
    own = jax.random.normal(subkeys[0], (HEADS, HD, D), jnp.float32)
    mixed = jnp.clip(own, -4.0, 4.0)
    scaled = mixed * (1.0 / math.sqrt(HEADS * HD))
    return scaled.reshape(HEADS * HD, D).astype(jnp.bfloat16)


def draw_query_blocks(key, part):
    key = jax.random.fold_in(key, 5)
    subkeys = jax.random.split(key, 2)
    stride = BPS // QB_DEV
    jitter = jax.random.randint(subkeys[0], (N_BLK, QB_DEV), 0, stride)
    jitter = jitter.at[0, 0].set(0).at[N_BLK - 1, QB_DEV - 1].set(stride - 1)
    blocks = jnp.arange(N_BLK, dtype=jnp.int32)[:, None] * BPS + jnp.arange(QB_DEV, dtype=jnp.int32)[None, :] * stride + jitter
    orders = jax.vmap(lambda sub: jax.random.permutation(sub, QB_DEV))(jax.random.split(subkeys[1], N_BLK))
    blocks = jnp.take_along_axis(blocks, orders, axis=1)
    return blocks.reshape(-1).astype(jnp.int32)


def block_scale(rng, extent, shards, least, high):
    def one(dim, shards_of):
        heights = jax.random.uniform(jax.random.fold_in(jax.random.fold_in(rng, 6), dim), (shards_of,), jnp.float32, least / len(shards), high / len(shards))
        return jnp.repeat(jnp.exp(heights), extent[dim] // shards_of).reshape((-1,) + (1,) * (len(extent) - dim - 1))

    factor_of = one(*shards[0])
    for cut in shards[1:]:
        factor_of = factor_of * one(*cut)
    return factor_of


def gaussian(rng, dims, deviation, bound, cuts=(), kind=jnp.bfloat16):
    values = deviation * jax.random.normal(rng, dims, jnp.float32)
    if cuts:
        values = values * block_scale(rng, dims, cuts, -0.22, 0.18)
    return jnp.clip(values, -bound, bound).astype(kind)


def setup_inputs(seed: int = 0) -> dict:
    seeds = jax.random.split(jax.random.key(seed), 12)
    qkv = draw_qkv(jax.random.fold_in(seeds[11], 71), 0)
    query_blocks = draw_query_blocks(jax.random.fold_in(seeds[11], 71), 0)
    out_weight = draw_out_weight(jax.random.fold_in(seeds[11], 71), 0)
    mod_shift = gaussian(seeds[3], (D,), 0.5, 3.0, (), jnp.float32)
    mod_scale = gaussian(seeds[4], (D,), 0.5, 3.0, (), jnp.float32)
    final_weight = gaussian(seeds[5], (D, PCH), D ** -0.5, 0.109375)
    final_bias = gaussian(seeds[6], (PCH,), 0.5, 3.0, (), jnp.float32)
    conv_in_weight = gaussian(seeds[7], (3, 3, 3, LAT, CH), (27 * LAT) ** -0.5, 0.3125)
    conv_in_bias = gaussian(seeds[8], (CH,), 0.5, 3.0, (), jnp.float32)
    conv_weight = gaussian(seeds[9], (3, 3, 3, CH, CH), (27 * CH) ** -0.5, 0.0546875, ((4, 16),))
    conv_bias = gaussian(seeds[10], (CH,), 0.5, 3.0, (), jnp.float32)
    return {"qkv": qkv, "query_blocks": query_blocks, "out_weight": out_weight, "mod_shift": mod_shift, "mod_scale": mod_scale, "final_weight": final_weight, "final_bias": final_bias, "conv_in_weight": conv_in_weight, "conv_in_bias": conv_in_bias, "conv_weight": conv_weight, "conv_bias": conv_bias}


def pad_field(field):
    padded = jnp.concatenate([field[:1], field[:1], field], axis=0)
    return jnp.pad(padded, ((0, 0), (1, 1), (1, 1), (0, 0)))

def convolve(padded, weight):
    frames = padded.shape[0] - 2
    height = padded.shape[1] - 2
    breadth = padded.shape[2] - 2
    summed = jnp.zeros((frames, height, breadth, weight.shape[4]), jnp.float32)
    for tap_time in range(3):
        for tap_row in range(3):
            for tap_col in range(3):
                window = padded[tap_time:tap_time + frames, tap_row:tap_row + height, tap_col:tap_col + breadth]
                flat = window.reshape(-1, window.shape[3])
                product = jnp.dot(flat, weight[tap_time, tap_row, tap_col], preferred_element_type=jnp.float32)
                summed = summed + product.reshape(frames, height, breadth, weight.shape[4])
    return summed

def reference(qkv, query_blocks, out_weight, mod_shift, mod_scale, final_weight, final_bias, conv_in_weight, conv_in_bias, conv_weight, conv_bias):
    by_head = qkv.reshape(S, 3, HEADS, HD)
    query_rows = (query_blocks[:, None] * QBLK + jnp.arange(QBLK, dtype=jnp.int32)[None, :]).reshape(-1).astype(jnp.int32)
    queries = jnp.take(by_head[:, 0], query_rows, axis=0)
    query_heads = jnp.transpose(queries, (1, 0, 2))
    key_heads = jnp.transpose(by_head[:, 1], (1, 0, 2))
    value_heads = jnp.transpose(by_head[:, 2], (1, 0, 2))
    inverse_root = 1.0 / math.sqrt(HD)

    def attend(triple):
        query_part, key_part, value_part = triple
        grouped = query_part.reshape(N_BLK, QPB, HD)

        def one_group(group_rows):
            scores = jnp.dot(group_rows, key_part.T, preferred_element_type=jnp.float32) * inverse_root
            highest = lax.optimization_barrier(jnp.max(scores, axis=1, keepdims=True))
            weights = jnp.exp(scores - highest)
            totals = lax.optimization_barrier(jnp.sum(weights, axis=1, keepdims=True))
            mixed = jnp.dot(weights.astype(jnp.bfloat16), value_part, preferred_element_type=jnp.float32)
            return (mixed / totals).astype(jnp.bfloat16)
        return lax.map(one_group, grouped).reshape(-1, HD)
    attended = lax.map(attend, (query_heads, key_heads, value_heads))
    attended = jnp.transpose(attended, (1, 0, 2)).reshape(-1, HEADS * HD)
    projected = jnp.dot(attended, out_weight, preferred_element_type=jnp.float32)
    average = lax.optimization_barrier(jnp.mean(projected, axis=1, keepdims=True))
    centred = projected - average
    spread = lax.optimization_barrier(jnp.mean(centred * centred, axis=1, keepdims=True))
    normed = centred * lax.rsqrt(spread + 1e-06)
    modulated = (normed * (1.0 + mod_scale) + mod_shift).astype(jnp.bfloat16)
    patches = (jnp.dot(modulated, final_weight, preferred_element_type=jnp.float32) + final_bias).astype(jnp.bfloat16)
    latent = patches.reshape(N_BLK, N_HEAD, TF, TH, TW, LAT, 2, 2)
    latent = jnp.transpose(latent, (2, 0, 3, 6, 1, 4, 7, 5)).reshape(TF, LH, LW, LAT)
    hidden = convolve(pad_field(latent), conv_in_weight) + conv_in_bias
    features = jax.nn.silu(hidden).astype(jnp.bfloat16)
    result = convolve(pad_field(features), conv_weight) + conv_bias
    return result.astype(jnp.bfloat16)
```

```python
import functools
import math

import jax
import jax.numpy as jnp
from jax import lax
from jax.experimental import pallas as pl
from jax.experimental.pallas import tpu as pltpu
from jax.sharding import PartitionSpec as P

HEADS = 16
HD = 128
D = 3072
QBLK = 128
QROWS = 512
CH = 512
NORM_EPS = 1e-06
BF = jnp.bfloat16
F32 = jnp.float32
COEF = math.log2(math.e) / math.sqrt(HD)
VMEM = 56 * 2**20

N = 16
GROUPS_XY = [[c + 2 * k for k in range(8)] for c in range(2)]
GROUPS_Z = [[x + 2 * k for k in range(8)] for x in range(2)]
CORE_SWAP = [(i, i ^ 1) for i in range(N)]


def ones_call(body, out_shape, scratch=(), name=None):
    return pl.pallas_call(
        body,
        out_shape=out_shape,
        scratch_shapes=scratch,
        compiler_params=pltpu.CompilerParams(vmem_limit_bytes=VMEM),
        name=name,
    )


def attention_body(sub, q_ref, own_ref, other_ref, o_ref, keys, vals):
    half = own_ref.shape[0]

    @pl.when(pl.program_id(0) == 0)
    def _():
        for s, ref in enumerate((own_ref, other_ref)):
            rows = pl.ds(s * half, half)
            keys[rows, :HD] = ref[:, :HD]
            keys[rows, HD:] = ref[:, :HD]
            vals[rows, :HD] = ref[:, HD:]
            vals[rows, HD:] = jnp.ones((half, HD), BF)

    def scores(i):
        q = q_ref[0, pl.ds(i * sub, sub), :].astype(F32) * COEF
        hi = q.astype(BF)
        lo = (q - hi.astype(F32)).astype(BF)
        return lax.dot_general(
            jnp.concatenate([hi, lo], axis=1),
            keys[...],
            (((1,), (1,)), ((), ())),
            preferred_element_type=F32,
        )

    lse_rows = []
    current = scores(0)
    for i in range(QROWS // sub):
        later = scores(i + 1) if (i + 1) * sub < QROWS else None
        high = jnp.max(current, axis=1, keepdims=True)
        weights = jnp.exp2(current - high).astype(BF)
        acc = jnp.dot(weights, vals[...], preferred_element_type=F32)
        total = acc[:, HD:]
        o_ref[0, pl.ds(i * sub, sub), :] = (acc[:, :HD] / total).astype(BF)
        lse = high + jnp.log2(total)
        for k in range(sub // 128):
            lse_rows.append(jnp.transpose(lse[k * 128 : (k + 1) * 128])[:1])
        current = later
    lse = jnp.concatenate(lse_rows, axis=0)
    hi = lse.astype(BF).astype(F32)
    mid = (lse - hi).astype(BF).astype(F32)
    low = lse - hi - mid
    tail = jnp.concatenate([hi, mid, low, jnp.zeros_like(hi)], axis=0)
    o_ref[0, QROWS:, :] = tail.astype(BF)


def attention(queries, own, other):
    chunks = queries.shape[0]
    half = own.shape[0]
    whole = pl.BlockSpec((half, 2 * HD), lambda i: (0, 0))
    return pl.pallas_call(
        functools.partial(attention_body, 256),
        grid=(chunks,),
        in_specs=[pl.BlockSpec((1, QROWS, HD), lambda i: (i, 0, 0)), whole, whole],
        out_specs=pl.BlockSpec((1, QROWS + 16, HD), lambda i: (i, 0, 0)),
        out_shape=jax.ShapeDtypeStruct((chunks, QROWS + 16, HD), BF),
        scratch_shapes=[pltpu.VMEM((2 * half, 2 * HD), BF), pltpu.VMEM((2 * half, 2 * HD), BF)],
        compiler_params=pltpu.CompilerParams(vmem_limit_bytes=VMEM),
        name="attention",
    )(queries, own, other)


def merge_body(part_ref, o_ref):
    count = part_ref.shape[0]
    lses = []
    for s in range(count):
        tail = part_ref[s, QROWS:, :].astype(F32)
        lses.append(tail[0:4] + tail[4:8] + tail[8:12])
    high = functools.reduce(jnp.maximum, lses)
    shares = [jnp.exp2(v - high) for v in lses]
    total = functools.reduce(jnp.add, shares)
    shares = [v / total for v in shares]
    for k in range(4):
        acc = jnp.zeros((128, HD), F32)
        for s in range(count):
            column = jnp.transpose(jnp.broadcast_to(shares[s][k : k + 1], (128, 128)))
            acc = acc + column * part_ref[s, pl.ds(k * 128, 128), :].astype(F32)
        o_ref[pl.ds(k * 128, 128), :] = acc.astype(BF)


def merge(parts):
    return ones_call(merge_body, jax.ShapeDtypeStruct((QROWS, HD), BF), name="merge")(parts)


def patch_body(att_ref, wa_ref, wb_ref, scale_ref, shift_ref, fw_ref, fb_ref, o_ref, rows, x):
    step = pl.program_id(0)
    cols = wa_ref.shape[1]

    @pl.when(step == 0)
    def _():
        for h in range(HEADS):
            rows[:, h * HD : (h + 1) * HD] = att_ref[h]

    a = rows[...]
    x[0, step] = jnp.dot(a, wa_ref[...], preferred_element_type=F32)
    x[1, step] = jnp.dot(a, wb_ref[...], preferred_element_type=F32)

    @pl.when(step == pl.num_programs(0) - 1)
    def _():
        steps = x.shape[1]
        parts = [x[s, i] for s in range(2) for i in range(steps)]
        mean = sum(jnp.sum(p, axis=1, keepdims=True) for p in parts) * (1.0 / D)
        parts = [p - mean for p in parts]
        var = sum(jnp.sum(p * p, axis=1, keepdims=True) for p in parts) * (1.0 / D)
        rstd = lax.rsqrt(var + NORM_EPS)
        acc = jnp.zeros(o_ref.shape, F32)
        for n, p in enumerate(parts):
            span = pl.ds(n * cols, cols)
            m = (p * rstd * (1.0 + scale_ref[:, span]) + shift_ref[:, span]).astype(BF)
            acc = acc + jnp.dot(m, fw_ref[span, :], preferred_element_type=F32)
        o_ref[...] = (acc + fb_ref[...]).astype(BF)


def patch_rows(att, wa, wb, scale, shift, fw, fb):
    half = wa.shape[1]
    cols = 512
    steps = half // cols
    block = pl.BlockSpec((HEADS * HD, cols), lambda i: (0, i))

    def whole(arr):
        return pl.BlockSpec(arr.shape, lambda i: (0,) * arr.ndim)

    count = att.shape[1]
    return pl.pallas_call(
        patch_body,
        grid=(steps,),
        in_specs=[whole(att), block, block, whole(scale), whole(shift), whole(fw), whole(fb)],
        out_specs=pl.BlockSpec((count, fw.shape[1]), lambda i: (0, 0)),
        out_shape=jax.ShapeDtypeStruct((count, fw.shape[1]), BF),
        scratch_shapes=[
            pltpu.VMEM((count, HEADS * HD), BF),
            pltpu.VMEM((2, steps, count, cols), F32),
        ],
        compiler_params=pltpu.CompilerParams(vmem_limit_bytes=VMEM),
        name="patches",
    )(att, wa, wb, scale, shift, fw, fb)


def conv_body(e_ref, w1_ref, b1_ref, mask_ref, w2_ref, b2_ref, o_ref, feat):
    wide = 512
    for j in range(2):
        lhs = jnp.concatenate([e_ref[j, a : a + 8] for a in range(3)], axis=-1)
        lhs = lhs.reshape(8 * 3 * 16, lhs.shape[-1])
        for n in range(2048 // wide):
            span = pl.ds(n * wide, wide)
            v = jnp.dot(lhs, w1_ref[:, span], preferred_element_type=F32) + b1_ref[:, span]
            v = v / (1.0 + jnp.exp(-v))
            v = v.reshape(8, 3, 16, wide) * mask_ref[:, :, span][None]
            v = v.astype(BF)
            feat[j, 2:, :, :, span] = v
            feat[j, 0, :, :, span] = v[0]
            feat[j, 1, :, :, span] = v[0]
    lane = lax.broadcasted_iota(jnp.int32, (128, 128), 1)
    col = lax.broadcasted_iota(jnp.int32, (128, 128), 0) % 16
    for y in range(4):
        acc = jnp.zeros((256, 128), F32)
        for a in range(3):
            for b in range(3):
                r, ey = divmod(y + b, 2)
                lhs = feat[:, a : a + 8, r, :, pl.ds(ey * 1024, 1024)].reshape(256, 1024)
                acc = acc + jnp.dot(lhs, w2_ref[a * 3 + b], preferred_element_type=F32)
        z0, z1 = acc[:128], acc[128:]
        right = jnp.where(col == 0, 0.0, pltpu.roll(z1, 1, 0))
        left = jnp.where(col == 15, 0.0, pltpu.roll(z0, 127, 0))
        s0 = z0 + pltpu.roll(jnp.where(lane < 96, right, z1), 64, 1)
        s1 = z1 + pltpu.roll(jnp.where(lane < 96, z0, left), 64, 1)
        out = jnp.where(lane < 64, s0, pltpu.roll(s1, 64, 1)) + b2_ref[...]
        o_ref[y] = out.astype(BF).reshape(8, 16, 128)


def conv_stage(e, w1, b1, mask, w2, b2):
    return ones_call(
        conv_body,
        jax.ShapeDtypeStruct((4, 8, 16, 128), BF),
        [pltpu.VMEM((2, 10, 3, 16, 2048), BF)],
        name="convs",
    )(e, w1, b1, mask, w2, b2)


def first_weights(k):
    outs = []
    for ey in range(2):
        for ex in range(2):
            wide = jnp.pad(k, ((0, 0), (ey, 1 - ey), (ex + 1, 2 - ex), (0, 0), (0, 0)))
            wide = wide.reshape(3, 2, 2, 3, 2, 16, CH)
            outs.append(jnp.transpose(wide, (0, 1, 3, 5, 2, 4, 6)).reshape(3 * 2 * 3 * 64, CH))
    return jnp.concatenate(outs, axis=1)


def second_weights(k):
    g = [k[:, :, i] for i in range(3)]
    none = jnp.zeros_like(g[0])
    even = jnp.concatenate([g[1], g[0], none, g[2]], axis=-1)
    odd = jnp.concatenate([g[2], g[1], g[0], none], axis=-1)
    return jnp.concatenate([even, odd], axis=2).reshape(9, 2 * CH, 128)


def window(rows):
    field = jnp.transpose(rows, (1, 2, 0, 3))
    zero = jnp.zeros_like(field[:, :, :1, :64])
    before = jnp.concatenate([zero, field[:, :, :-1, 64:]], axis=2)
    after = jnp.concatenate([field[:, :, 1:, :64], zero], axis=2)
    both = jnp.stack(
        [jnp.concatenate([before, field], axis=-1), jnp.concatenate([field, after], axis=-1)]
    )
    pairs = jnp.concatenate([both[:, :, :3], both[:, :, 1:]], axis=-1)
    return jnp.concatenate([pairs[:, :1], pairs[:, :1], pairs], axis=1)


def shards(
    qkv,
    query_blocks,
    out_weight,
    mod_shift,
    mod_scale,
    final_weight,
    final_bias,
    conv_in_weight,
    conv_in_bias,
    conv_weight,
    conv_bias,
):
    head = lax.axis_index("head")
    blk = lax.axis_index("blk")
    core = blk % 2
    tok = qkv.shape[1]

    parts = qkv.reshape(tok, 3, HEADS, HD)
    q_send = jnp.transpose(parts[:, 0], (1, 0, 2))
    kv_send = jnp.concatenate([parts[:, 1], parts[:, 2]], axis=-1)
    kv_send = jnp.transpose(kv_send, (1, 0, 2))
    q_all = lax.all_to_all(q_send, "head", 0, 0, tiled=True)
    kv_own = lax.all_to_all(kv_send, "head", 0, 0, tiled=True).reshape(-1, 2 * HD)

    half = lax.dynamic_slice_in_dim(out_weight, core * (D // 2), D // 2, axis=1)
    paired = lax.ppermute(half, "head", CORE_SWAP)
    even = (head % 2) == 0
    pair = jnp.stack([jnp.where(even, half, paired), jnp.where(even, paired, half)])
    weight_a = lax.all_gather(pair, "head", axis=0, tiled=True, axis_index_groups=GROUPS_Z)
    weight_a = weight_a.reshape(HEADS * HD, D // 2)
    weight_b = lax.ppermute(weight_a, "blk", CORE_SWAP)

    chosen = query_blocks % N
    queries = jnp.take(q_all.reshape(N, QBLK, HD), chosen, axis=0).reshape(1, QROWS, HD)
    queries = lax.all_to_all(
        jnp.broadcast_to(queries, (8, QROWS, HD)),
        "blk",
        0,
        0,
        tiled=True,
        axis_index_groups=GROUPS_XY,
    )
    kv_other = lax.ppermute(kv_own, "blk", CORE_SWAP)
    partial = attention(queries, kv_own, kv_other)
    partial = lax.all_to_all(partial, "blk", 0, 0, tiled=True, axis_index_groups=GROUPS_XY)
    attended = merge(partial).reshape(N, QROWS // N, HD)
    attended = lax.all_to_all(attended, "head", 0, 0, tiled=True)

    def own_first(arr, axis):
        return jnp.where(core == 0, arr, jnp.roll(arr, D // 2, axis=axis))

    patches = patch_rows(
        attended,
        weight_a,
        weight_b,
        own_first(mod_scale.reshape(1, D), 1),
        own_first(mod_shift.reshape(1, D), 1),
        own_first(final_weight, 0),
        final_bias.reshape(1, -1),
    )

    tile = patches.reshape(8, 2, 128)
    ends = N - 1
    above = lax.ppermute(tile[:, 1:], "blk", [(i, i + 1) for i in range(ends)])
    below = lax.ppermute(tile[:, :1], "blk", [(i + 1, i) for i in range(ends)])
    rows = jnp.concatenate([above, tile, below], axis=1)
    rows = lax.all_to_all(
        jnp.broadcast_to(rows[None], (N,) + rows.shape), "head", 0, 0, tiled=True
    )

    inside = jnp.ones((3, 2, 2 * CH), F32)
    inside = inside.at[0, 0].set(jnp.where(blk == 0, 0.0, 1.0))
    inside = inside.at[2, 1].set(jnp.where(blk == N - 1, 0.0, 1.0))
    bias_out = lax.dynamic_slice_in_dim(conv_bias, head * 32, 32)
    out = conv_stage(
        window(rows),
        first_weights(conv_in_weight),
        jnp.tile(conv_in_bias, 4).reshape(1, -1),
        inside.reshape(3, 1, 4 * CH),
        second_weights(conv_weight),
        jnp.tile(bias_out, 4).reshape(1, -1),
    )
    out = lax.all_to_all(jnp.transpose(out, (2, 0, 1, 3)), "head", 0, 0, tiled=True)
    out = jnp.transpose(out.reshape(N, 4, 8, 4, 32), (2, 1, 3, 0, 4))
    return out.reshape(8, 4, 4, CH)


def solution(mesh):
    in_specs = (
        P("blk", "head", None),
        P("blk"),
        P("head", None),
        P(),
        P(),
        P(),
        P(),
        P(),
        P(),
        P(None, None, None, None, "head"),
        P(),
    )
    out_specs = P(None, "blk", "head", None)
    return jax.shard_map(shards, mesh=mesh, in_specs=in_specs, out_specs=out_specs, check_vma=False)
```

```python
import functools
import math

import jax
import jax.numpy as jnp
from jax import lax
from jax.experimental import pallas as pl
from jax.experimental.pallas import tpu as pltpu
from jax.sharding import PartitionSpec as P

HEADS = 16
HD = 128
D = 3072
QBLK = 128
QROWS = 512
CH = 512
NORM_EPS = 1e-06
BF = jnp.bfloat16
F32 = jnp.float32
COEF = math.log2(math.e) / math.sqrt(HD)
MIB = 2**20

N = 16
GROUPS_Z = [[x + 2 * k for k in range(8)] for x in range(2)]
GROUPS_Y = [[x * 8 + c + 2 * k for k in range(4)] for x in range(2) for c in range(2)]
NEXT_SWAP = [(i, i ^ 1) for i in range(N)]
FAR_SWAP = [(i, i ^ 8) for i in range(N)]


def ones_call(body, out_shape, scratch=(), name=None):
    return pl.pallas_call(
        body,
        out_shape=out_shape,
        scratch_shapes=scratch,
        compiler_params=pltpu.CompilerParams(vmem_limit_bytes=32 * MIB),
        name=name,
    )


def split_body(x_ref, q_ref, kv_ref):
    for h in range(HEADS):
        q_ref[h] = x_ref[0, :, pl.ds(h * HD, HD)]
        for part in (1, 2):
            span = pl.ds((part * HEADS + h) * HD, HD)
            kv_ref[h, :, pl.ds((part - 1) * HD, HD)] = x_ref[0, :, span]


def split_heads(qkv):
    tok = qkv.shape[1]
    shapes = [jax.ShapeDtypeStruct((HEADS, tok, k * HD), BF) for k in (1, 2)]
    return ones_call(split_body, shapes, name="split")(qkv)


def select_body(chosen_ref, q_ref, o_ref):
    for i in range(QROWS // QBLK):
        o_ref[pl.ds(i * QBLK, QBLK), :] = q_ref[chosen_ref[i] % N]


def select_queries(chosen, q_all):
    return pl.pallas_call(
        select_body,
        in_specs=[
            pl.BlockSpec(memory_space=pltpu.SMEM),
            pl.BlockSpec(memory_space=pltpu.VMEM),
        ],
        out_shape=jax.ShapeDtypeStruct((QROWS, HD), BF),
        name="select",
    )(chosen, q_all)


def store_lse(o_ref, lse):
    hi = lse.astype(BF).astype(F32)
    mid = (lse - hi).astype(BF).astype(F32)
    low = lse - hi - mid
    tail = jnp.concatenate([hi, mid, low, jnp.zeros_like(hi)], axis=0)
    o_ref[0, QROWS:, :] = tail.astype(BF)


def load_lse(ref, s):
    tail = ref[s, QROWS:, :].astype(F32)
    return tail[0:4] + tail[4:8] + tail[8:12]


def column(row):
    return jnp.transpose(jnp.broadcast_to(row, (128, 128)))


def attention_body(sub, place_ref, *refs):
    q_refs, (own_ref, other_ref, o_ref, keys, vals, q_now) = refs[:4], refs[4:]
    half = own_ref.shape[0]
    for m, q_ref in enumerate(q_refs):

        @pl.when(pl.program_id(0) == m)
        def _(q_ref=q_ref):
            q_now[...] = q_ref[...]

    @pl.when(pl.program_id(0) == 0)
    def _():
        for s, ref in enumerate((own_ref, other_ref)):
            rows = pl.ds(s * half, half)
            keys[rows, :HD] = ref[:, :HD]
            keys[rows, HD:] = ref[:, :HD]
            vals[rows, :HD] = ref[:, HD:]
            vals[rows, HD:] = jnp.ones((half, HD), BF)

    def scores(i):
        q = q_now[pl.ds(i * sub, sub), :].astype(F32) * COEF
        hi = q.astype(BF)
        lo = (q - hi.astype(F32)).astype(BF)
        return lax.dot_general(
            jnp.concatenate([hi, lo], axis=1),
            keys[...],
            (((1,), (1,)), ((), ())),
            preferred_element_type=F32,
        )

    lse_rows = []
    current = scores(0)
    for i in range(QROWS // sub):
        later = scores(i + 1) if (i + 1) * sub < QROWS else None
        high = jnp.max(current, axis=1, keepdims=True)
        weights = jnp.exp2(current - high).astype(BF)
        acc = jnp.dot(weights, vals[...], preferred_element_type=F32)
        total = acc[:, HD:]
        o_ref[0, pl.ds(i * sub, sub), :] = (acc[:, :HD] / total).astype(BF)
        lse = high + jnp.log2(total)
        for k in range(sub // 128):
            lse_rows.append(jnp.transpose(lse[k * 128 : (k + 1) * 128])[:1])
        current = later
    store_lse(o_ref, jnp.concatenate(lse_rows, axis=0))


def attention(part, place, queries, own, other):
    half = own.shape[0]
    whole = pl.BlockSpec((half, 2 * HD), lambda i, place: (0, 0))
    rows = pl.BlockSpec((QROWS, HD), lambda i, place: (part, 0))
    return pl.pallas_call(
        functools.partial(attention_body, 256),
        grid_spec=pltpu.PrefetchScalarGridSpec(
            num_scalar_prefetch=1,
            grid=(4,),
            in_specs=[rows] * 4 + [whole, whole],
            out_specs=pl.BlockSpec(
                (1, QROWS + 16, HD), lambda i, place: (place[0] ^ i, 0, 0)
            ),
            scratch_shapes=[pltpu.VMEM((2 * half, 2 * HD), BF)] * 2
            + [pltpu.VMEM((QROWS, HD), BF)],
        ),
        out_shape=jax.ShapeDtypeStruct((4, QROWS + 16, HD), BF),
        compiler_params=pltpu.CompilerParams(vmem_limit_bytes=32 * MIB),
        cost_estimate=pl.CostEstimate(
            flops=4 * 4 * QROWS * 2 * half * 2 * HD,
            bytes_accessed=4 * MIB,
            transcendentals=4 * QROWS * 2 * half,
        ),
        name="attention",
    )(place, *queries, own, other)


def merge_two_body(a_ref, b_ref, o_ref):
    la, lb = load_lse(a_ref, 0), load_lse(b_ref, 0)
    high = jnp.maximum(la, lb)
    ea, eb = jnp.exp2(la - high), jnp.exp2(lb - high)
    total = ea + eb
    store_lse(o_ref, high + jnp.log2(total))
    ea, eb = ea / total, eb / total
    for k in range(4):
        span = pl.ds(k * 128, 128)
        mixed = column(ea[k : k + 1]) * a_ref[0, span, :].astype(F32)
        mixed = mixed + column(eb[k : k + 1]) * b_ref[0, span, :].astype(F32)
        o_ref[0, span, :] = mixed.astype(BF)


def merge_two(a, b):
    block = pl.BlockSpec((1,) + a.shape[1:], lambda i: (i, 0, 0))
    return pl.pallas_call(
        merge_two_body,
        grid=(a.shape[0],),
        in_specs=[block, block],
        out_specs=block,
        out_shape=jax.ShapeDtypeStruct(a.shape, BF),
        name="merge_two",
    )(a, b)


def merge_body(part_ref, o_ref):
    count = part_ref.shape[0]
    lses = [load_lse(part_ref, s) for s in range(count)]
    high = functools.reduce(jnp.maximum, lses)
    shares = [jnp.exp2(v - high) for v in lses]
    total = functools.reduce(jnp.add, shares)
    shares = [v / total for v in shares]
    for k in range(4):
        acc = jnp.zeros((128, HD), F32)
        for s in range(count):
            part = part_ref[s, pl.ds(k * 128, 128), :].astype(F32)
            acc = acc + column(shares[s][k : k + 1]) * part
        acc = acc.astype(BF)
        for n in range(4):
            o_ref[k * 4 + n] = acc[n // 2 * 64 : n // 2 * 64 + 64]


def merge(parts):
    return ones_call(merge_body, jax.ShapeDtypeStruct((N, 64, HD), BF), name="merge")(parts)


def bf16_terms(v):
    hi = v.astype(BF).astype(F32)
    mid = (v - hi).astype(BF).astype(F32)
    return [hi, mid, v - hi - mid]


def project_body(
    pos_ref, att_ref, wa_ref, wb_ref, scale_ref, shift_ref, fw_ref, fb_ref, *refs
):
    own_ref, send_ref, const_ref, rows, x, stats = refs
    step = pl.program_id(0)
    core, side = pos_ref[0], pos_ref[1]
    cols = wa_ref.shape[1]
    half = D // 2
    contract = (((1,), (1,)), ((), ()))

    @pl.when(step == 0)
    def _():
        for h in range(HEADS):
            rows[:, h * HD : (h + 1) * HD] = att_ref[h]
        moved = jnp.zeros((1, 128), F32)
        blank = jnp.zeros((64, half), BF)
        for s in range(2):
            span = pl.ds(s * half, half)
            terms = bf16_terms(1.0 + scale_ref[:, span]) + bf16_terms(shift_ref[:, span])
            lhs = jnp.concatenate(terms + [jnp.zeros((2, half), F32)], axis=0).astype(BF)
            rhs = jnp.concatenate([fw_ref[:, span], blank], axis=0)
            got = lax.dot_general(lhs, rhs, contract, preferred_element_type=F32)
            const_ref[s : s + 1, :] = got[0:1] + got[1:2] + got[2:3]
            moved = moved + got[3:4] + got[4:5] + got[5:6]
        const_ref[2:3, :] = moved + fb_ref[...]

    a = rows[...]
    x[core, step] = jnp.dot(a, wa_ref[...], preferred_element_type=F32)
    x[1 - core, step] = jnp.dot(a, wb_ref[...], preferred_element_type=F32)

    @pl.when(step == pl.num_programs(0) - 1)
    def _():
        parts = [x[s, i] for s in range(2) for i in range(x.shape[1])]
        mean = sum(jnp.sum(p, axis=1, keepdims=True) for p in parts) * (1.0 / half)
        parts = [p - mean for p in parts]
        square = sum(jnp.sum(p * p, axis=1, keepdims=True) for p in parts)
        acc = jnp.zeros(stats.shape, F32)
        blank = jnp.zeros((64, cols), BF)
        for n, p in enumerate(parts):
            span = pl.ds(pl.multiple_of(side * half, 128) + n * cols, cols)
            m = (p * (1.0 + scale_ref[:, span])).astype(BF)
            rhs = jnp.concatenate([fw_ref[:, span], blank], axis=0)
            acc = acc + lax.dot_general(m, rhs, contract, preferred_element_type=F32)
        lane = lax.broadcasted_iota(jnp.int32, stats.shape, 1)
        stats[...] = jnp.where(lane < 64, acc, jnp.where(lane < 96, mean, square))
        own_ref[...] = stats[pl.ds(pl.multiple_of(side * 32, 32), 32), :]
        send_ref[...] = stats[pl.ds(pl.multiple_of(32 - side * 32, 32), 32), :]


def project(pos, att, wa, wb, scale, shift, fw, fb):
    cols = 384
    steps = wa.shape[1] // cols
    block = pl.BlockSpec((HEADS * HD, cols), lambda i: (0, i))

    def whole(shape):
        return pl.BlockSpec(shape, lambda i: (0,) * len(shape))

    count = att.shape[1]
    outs = [(32, 128), (32, 128), (8, 128)]
    return pl.pallas_call(
        project_body,
        grid=(steps,),
        in_specs=[
            pl.BlockSpec(memory_space=pltpu.SMEM),
            whole(att.shape),
            block,
            block,
            whole(scale.shape),
            whole(shift.shape),
            whole(fw.shape),
            whole(fb.shape),
        ],
        out_specs=[whole(o) for o in outs],
        out_shape=[jax.ShapeDtypeStruct(o, F32) for o in outs],
        scratch_shapes=[
            pltpu.VMEM((count, HEADS * HD), BF),
            pltpu.VMEM((2, steps, count, cols), F32),
            pltpu.VMEM((count, 128), F32),
        ],
        compiler_params=pltpu.CompilerParams(vmem_limit_bytes=32 * MIB),
        name="project",
    )(pos, att, wa, wb, scale, shift, fw, fb)


def finish_body(pos_ref, own_ref, got_ref, const_ref, o_ref):
    side = pos_ref[1]
    own, got = own_ref[...], got_ref[...]
    m_own, m_got = own[:, 64:65], got[:, 64:65]
    apart = m_own - m_got
    square = own[:, 96:97] + got[:, 96:97] + apart * apart * (D / 4)
    rstd = lax.rsqrt(square * (1.0 / D) + NORM_EPS)
    first, second = const_ref[0:1, :], const_ref[1:2, :]
    u_own = jnp.where(side == 0, first, second)
    u_got = jnp.where(side == 0, second, first)
    total = own + got + (0.5 * apart) * (u_own - u_got)
    out = (total * rstd + const_ref[2:3, :]).astype(BF)[:, :64]

    src = lax.broadcasted_iota(jnp.int32, (64, 128), 0)
    dst = lax.broadcasted_iota(jnp.int32, (64, 128), 1)
    place = (src % 2) * 32 + (src // 2 % 2) * 16 + src // 4
    to = lax.broadcasted_iota(jnp.int32, (16, 32), 0)
    row = lax.broadcasted_iota(jnp.int32, (16, 32), 1)
    acc = jnp.zeros((16, 128), F32)
    for j in range(2):
        perm = jnp.where(dst == place + 64 * j, 1.0, 0.0).astype(BF)
        pick = jnp.where(row == (to % 8 * 2 + to // 8) * 2 + j, 1.0, 0.0).astype(BF)
        lanes = jnp.dot(out, perm, preferred_element_type=F32).astype(BF)
        acc = acc + jnp.dot(pick, lanes, preferred_element_type=F32)
    o_ref[...] = acc.astype(BF)


def finish(pos, own, got, const):
    vmem = pl.BlockSpec(memory_space=pltpu.VMEM)
    return pl.pallas_call(
        finish_body,
        in_specs=[pl.BlockSpec(memory_space=pltpu.SMEM), vmem, vmem, vmem],
        out_shape=jax.ShapeDtypeStruct((16, 128), BF),
        name="finish",
    )(pos, own, got, const)


def conv_body(blk_ref, r_ref, k1_ref, b1_ref, k2_ref, b2_ref, o_ref, win, feat, w1, w2):
    blank = jnp.zeros((16, CH), BF)
    for a in range(3):
        for wr in range(4):
            for wc in range(4):
                ry, p = divmod(wr, 2)
                row = ((a * 2 + ry) * 4 + wc) * 32 + p * 16
                for ey in range(2):
                    for ex in range(2):
                        b, g = wr - ey, wc - ex
                        hit = 0 <= b < 3 and 0 <= g < 3
                        tile = k1_ref[(a * 3 + b) * 3 + g] if hit else blank
                        w1[pl.ds(row, 16), pl.ds((ey * 2 + ex) * CH, CH)] = tile
    taps = ((1, 0, None, 2), (2, 1, 0, None))
    blank = jnp.zeros((32, CH), BF)
    for a in range(3):
        for u, pair in enumerate(((2, None), (1, 2), (0, 1), (None, 0))):
            for ey, b in enumerate(pair):
                for qi in range(2):
                    for n, g in enumerate(taps[qi]):
                        hit = b is not None and g is not None
                        tile = k2_ref[(a * 3 + b) * 3 + g] if hit else blank
                        span = pl.ds((ey * 2 + qi) * CH, CH)
                        w2[a, pl.ds(u * 128 + n * 32, 32), span] = tile

    rows = r_ref[...].astype(F32).reshape(512, 128)
    lane = lax.broadcasted_iota(jnp.int32, (512, 128), 1)
    col = lax.broadcasted_iota(jnp.int32, (512, 128), 0) % 16
    before = jnp.where(col == 0, 0.0, pltpu.roll(rows, 1, 0))
    after = jnp.where(col == 15, 0.0, pltpu.roll(rows, 511, 0))
    views = (
        pltpu.roll(jnp.where(lane < 96, rows, before), 32, 1),
        pltpu.roll(jnp.where(lane < 32, after, rows), 96, 1),
    )
    for j, view in enumerate(views):
        view = view.astype(BF).reshape(4, 8, 16, 128)
        for r in range(3):
            for ry in range(2):
                span = pl.ds(ry * 128, 128)
                win[j, 2:, r, :, span] = view[r + ry]
                for early in range(2):
                    win[j, early, r, :, span] = view[r + ry, 0]

    top = jnp.where(blk_ref[0] == 0, 0.0, 1.0)
    bottom = jnp.where(blk_ref[0] == N - 1, 0.0, 1.0)
    for j in range(2):
        lhs = jnp.concatenate([win[j, a : a + 8] for a in range(3)], axis=-1)
        lhs = lhs.reshape(8 * 3 * 16, lhs.shape[-1])
        for n in range(4):
            span = pl.ds(n * CH, CH)
            v = jnp.dot(lhs, w1[:, span], preferred_element_type=F32) + b1_ref[...]
            v = (v / (1.0 + jnp.exp(-v))).reshape(8, 3, 16, CH)
            for r in range(3):
                f = v[:, r]
                if (r, n // 2) == (0, 0):
                    f = f * top
                if (r, n // 2) == (2, 1):
                    f = f * bottom
                f = f.astype(BF)
                feat[j, 2:, r, :, span] = f
                feat[j, 0, r, :, span] = f[0]
                feat[j, 1, r, :, span] = f[0]

    def product(a, r, first):
        lhs = feat[:, a : a + 8, r].reshape(256, 4 * CH)
        rhs = w2[a, pl.ds(first, 256), :]
        return lax.dot_general(lhs, rhs, (((1,), (1,)), ((), ())), preferred_element_type=F32)

    lane = lax.broadcasted_iota(jnp.int32, (128, 128), 1)
    col = lax.broadcasted_iota(jnp.int32, (128, 128), 0) % 16
    for pair in range(2):
        acc = jnp.zeros((256, 256), F32)
        for a in range(3):
            acc = acc + product(a, pair, 256) + product(a, pair + 1, 0)
        for y in range(2):
            z = acc[:, y * 128 : (y + 1) * 128]
            z0, z1 = z[:128], z[128:]
            right = jnp.where(col == 0, 0.0, pltpu.roll(z1, 1, 0))
            left = jnp.where(col == 15, 0.0, pltpu.roll(z0, 127, 0))
            s0 = z0 + pltpu.roll(jnp.where(lane < 96, right, z1), 64, 1)
            s1 = z1 + pltpu.roll(jnp.where(lane < 96, z0, left), 64, 1)
            out = jnp.where(lane < 64, s0, pltpu.roll(s1, 64, 1)) + b2_ref[...]
            o_ref[pair * 2 + y] = out.astype(BF).reshape(8, 16, 128)


def conv_stage(blk, rows, k1, b1, k2, b2):
    vmem = pl.BlockSpec(memory_space=pltpu.VMEM)
    return pl.pallas_call(
        conv_body,
        in_specs=[pl.BlockSpec(memory_space=pltpu.SMEM)] + [vmem] * 5,
        out_shape=jax.ShapeDtypeStruct((4, 8, 16, 128), BF),
        scratch_shapes=[
            pltpu.VMEM((2, 10, 3, 16, 256), BF),
            pltpu.VMEM((2, 10, 3, 16, 4 * CH), BF),
            pltpu.VMEM((768, 4 * CH), BF),
            pltpu.VMEM((3, 512, 4 * CH), BF),
        ],
        compiler_params=pltpu.CompilerParams(vmem_limit_bytes=32 * MIB),
        name="convs",
    )(blk, rows, k1, b1, k2, b2)


def after(value, *others):
    return lax.optimization_barrier((value,) + others)[0]


def shards(
    qkv,
    query_blocks,
    out_weight,
    mod_shift,
    mod_scale,
    final_weight,
    final_bias,
    conv_in_weight,
    conv_in_bias,
    conv_weight,
    conv_bias,
):
    head = lax.axis_index("head")
    blk = lax.axis_index("blk")
    core = blk % 2
    side = head % 2
    pos = jnp.stack([core, side])

    q_send, kv_send = split_heads(qkv)
    q_all = lax.all_to_all(q_send, "head", 0, 0, tiled=True)
    kv_own = lax.all_to_all(after(kv_send, q_all), "head", 0, 0, tiled=True)
    kv_own = kv_own.reshape(-1, 2 * HD)

    near = select_queries(query_blocks, q_all)
    both = jnp.concatenate([near, lax.ppermute(near, "blk", FAR_SWAP)], axis=0)
    queries = [both]
    for m in range(1, 4):
        swap = [(i, i ^ (2 * m)) for i in range(N)]
        queries.append(lax.ppermute(both, "blk", swap))
    kv_own = after(kv_own, *queries)
    kv_other = lax.ppermute(kv_own, "blk", NEXT_SWAP)

    quarter = D // 4
    mine, theirs = (side * 2 + core) * quarter, ((1 - side) * 2 + core) * quarter
    source = after(out_weight, q_send)
    part = lax.dynamic_slice_in_dim(source, mine, quarter, axis=1)
    given = lax.dynamic_slice_in_dim(source, theirs, quarter, axis=1)
    given = after(lax.ppermute(given, "head", NEXT_SWAP), q_all)
    pair = jnp.stack([jnp.where(side == 0, part, given), jnp.where(side == 0, given, part)])
    weight_a = lax.all_gather(pair, "head", axis=0, tiled=True, axis_index_groups=GROUPS_Z)

    place = (blk // 2 % 4).reshape(1)
    far_part = attention(1, place, queries, kv_own, kv_other)
    got_part = lax.ppermute(far_part, "blk", FAR_SWAP)
    near_part = attention(0, after(place, far_part), queries, kv_own, kv_other)
    partial = merge_two(near_part, got_part)

    weight_a = after(weight_a, far_part).reshape(HEADS * HD, quarter)
    weight_b = lax.ppermute(weight_a, "blk", NEXT_SWAP)

    partial = lax.all_to_all(partial, "blk", 0, 0, tiled=True, axis_index_groups=GROUPS_Y)
    attended = lax.all_to_all(merge(partial), "head", 0, 0, tiled=True)
    own, send, const = project(
        pos,
        attended,
        weight_a,
        weight_b,
        mod_scale.reshape(1, D),
        mod_shift.reshape(1, D),
        jnp.transpose(final_weight),
        jnp.pad(final_bias, (0, 64)).reshape(1, 128),
    )
    tile = finish(pos, own, lax.ppermute(send, "head", NEXT_SWAP), const)

    ends = N - 1
    above = lax.ppermute(tile[8:], "blk", [(i, i + 1) for i in range(ends)])
    below = lax.ppermute(tile[:8], "blk", [(i + 1, i) for i in range(ends)])
    rows = jnp.concatenate([above, tile, below], axis=0)
    rows = lax.all_to_all(
        jnp.broadcast_to(rows[None], (N,) + rows.shape), "head", 0, 0, tiled=True
    )
    bias_out = lax.dynamic_slice_in_dim(conv_bias, head * 32, 32)
    out = conv_stage(
        blk.reshape(1),
        jnp.transpose(rows, (1, 0, 2)),
        conv_in_weight.reshape(27, 16, CH),
        conv_in_bias.reshape(1, CH),
        jnp.transpose(conv_weight, (0, 1, 2, 4, 3)).reshape(27, 32, CH),
        jnp.tile(bias_out, 4).reshape(1, -1),
    )
    out = lax.all_to_all(jnp.transpose(out, (2, 0, 1, 3)), "head", 0, 0, tiled=True)
    out = jnp.transpose(out.reshape(N, 4, 8, 4, 32), (2, 1, 3, 0, 4))
    return out.reshape(8, 4, 4, CH)


def solution(mesh):
    in_specs = (
        P("blk", "head", None),
        P("blk"),
        P("head", None),
        P(),
        P(),
        P(),
        P(),
        P(),
        P(),
        P(None, None, None, None, "head"),
        P(),
    )
    out_specs = P(None, "blk", "head", None)
    return jax.shard_map(shards, mesh=mesh, in_specs=in_specs, out_specs=out_specs, check_vma=False)
```

```python
import functools
import math

import jax
import jax.numpy as jnp
from jax import lax
from jax.experimental import pallas as pl
from jax.experimental.pallas import tpu as pltpu
from jax.sharding import PartitionSpec as P

HEADS = 16
HD = 128
D = 3072
QBLK = 128
QROWS = 512
CH = 512
NORM_EPS = 1e-06
BF = jnp.bfloat16
F32 = jnp.float32
COEF = math.log2(math.e) / math.sqrt(HD)
MIB = 2**20

N = 16
GROUPS_Z = [[x + 2 * k for k in range(8)] for x in range(2)]
GROUPS_Y = [[x * 8 + c + 2 * k for k in range(4)] for x in range(2) for c in range(2)]
NEXT_SWAP = [(i, i ^ 1) for i in range(N)]
FAR_SWAP = [(i, i ^ 8) for i in range(N)]


def ones_call(body, out_shape, limit, name):
    return pl.pallas_call(
        body,
        out_shape=out_shape,
        compiler_params=pltpu.CompilerParams(vmem_limit_bytes=limit * MIB),
        name=name,
    )


def split_body(*refs):
    o_ref = refs[-1]
    for n, ref in enumerate(refs[:-1]):
        for h in range(HEADS):
            o_ref[h, :, n * HD : (n + 1) * HD] = ref[0, :, h * HD : (h + 1) * HD]


def split_heads(qkv, parts):
    tok = qkv.shape[1]
    return pl.pallas_call(
        split_body,
        grid=(1,),
        in_specs=[
            pl.BlockSpec((1, tok, HEADS * HD), lambda i, p=p: (0, 0, p)) for p in parts
        ],
        out_specs=pl.BlockSpec((HEADS, tok, len(parts) * HD), lambda i: (0, 0, 0)),
        out_shape=jax.ShapeDtypeStruct((HEADS, tok, len(parts) * HD), BF),
        compiler_params=pltpu.CompilerParams(vmem_limit_bytes=56 * MIB),
        name="split",
    )(*[qkv] * len(parts))


def select_body(chosen_ref, q_ref, o_ref):
    for i in range(QROWS // QBLK):
        o_ref[pl.ds(i * QBLK, QBLK), :] = q_ref[chosen_ref[i] % N]


def select_queries(chosen, q_all):
    return pl.pallas_call(
        select_body,
        in_specs=[
            pl.BlockSpec(memory_space=pltpu.SMEM),
            pl.BlockSpec(memory_space=pltpu.VMEM),
        ],
        out_shape=jax.ShapeDtypeStruct((QROWS, HD), BF),
        compiler_params=pltpu.CompilerParams(vmem_limit_bytes=4 * MIB),
        name="select",
    )(chosen, q_all)


def store_lse(o_ref, chunk, lse):
    hi = lse.astype(BF).astype(F32)
    mid = (lse - hi).astype(BF).astype(F32)
    low = lse - hi - mid
    tail = jnp.concatenate([hi, mid, low, jnp.zeros_like(hi)], axis=0)
    o_ref[chunk, QROWS:, :] = tail.astype(BF)


def load_lse(ref, s):
    tail = ref[s, QROWS:, :].astype(F32)
    return tail[0:4] + tail[4:8] + tail[8:12]


def column(row):
    return jnp.transpose(jnp.broadcast_to(row, (128, 128)))


def attention_body(sub, place_ref, *refs):
    q_refs, (own_ref, other_ref, o_ref, keys, vals) = refs[:4], refs[4:]
    half = own_ref.shape[0]
    for s, ref in enumerate((own_ref, other_ref)):
        rows = pl.ds(s * half, half)
        keys[rows, :HD] = ref[:, :HD]
        keys[rows, HD:] = ref[:, :HD]
        vals[rows, :HD] = ref[:, HD:]
        vals[rows, HD:] = jnp.ones((half, HD), BF)

    def scores(chunk, first):
        q = q_refs[chunk][first : first + sub, :].astype(F32) * COEF
        hi = q.astype(BF)
        lo = (q - hi.astype(F32)).astype(BF)
        return lax.dot_general(
            jnp.concatenate([hi, lo], axis=1),
            keys[...],
            (((1,), (1,)), ((), ())),
            preferred_element_type=F32,
        )

    tiles = [(chunk, first) for chunk in range(4) for first in range(0, QROWS, sub)]
    lse_rows = []
    current = scores(*tiles[0])
    for n, (chunk, first) in enumerate(tiles):
        later = scores(*tiles[n + 1]) if n + 1 < len(tiles) else None
        high = jnp.max(current, axis=1, keepdims=True)
        weights = jnp.exp2(current - high).astype(BF)
        acc = jnp.dot(weights, vals[...], preferred_element_type=F32)
        total = acc[:, HD:]
        to = place_ref[0] ^ chunk
        o_ref[to, first : first + sub, :] = (acc[:, :HD] / total).astype(BF)
        lse = high + jnp.log2(total)
        for k in range(sub // 128):
            lse_rows.append(jnp.transpose(lse[k * 128 : (k + 1) * 128])[:1])
        if first + sub == QROWS:
            store_lse(o_ref, to, jnp.concatenate(lse_rows, axis=0))
            lse_rows = []
        current = later


def attention(part, place, queries, own, other):
    half = own.shape[0]
    whole = pl.BlockSpec((half, 2 * HD), lambda i: (0, 0))
    rows = pl.BlockSpec((QROWS, HD), lambda i: (part, 0))
    return pl.pallas_call(
        functools.partial(attention_body, 256),
        grid=(1,),
        in_specs=[pl.BlockSpec(memory_space=pltpu.SMEM)] + [rows] * 4 + [whole, whole],
        out_specs=pl.BlockSpec((4, QROWS + 16, HD), lambda i: (0, 0, 0)),
        out_shape=jax.ShapeDtypeStruct((4, QROWS + 16, HD), BF),
        scratch_shapes=[pltpu.VMEM((2 * half, 2 * HD), BF)] * 2,
        compiler_params=pltpu.CompilerParams(vmem_limit_bytes=24 * MIB),
        cost_estimate=pl.CostEstimate(
            flops=4 * 4 * QROWS * 2 * half * 2 * HD,
            bytes_accessed=4 * MIB,
            transcendentals=4 * QROWS * 2 * half,
        ),
        name="attention",
    )(place, *queries, own, other)


def merge_two_body(a_ref, b_ref, o_ref):
    for n in range(a_ref.shape[0]):
        la, lb = load_lse(a_ref, n), load_lse(b_ref, n)
        high = jnp.maximum(la, lb)
        ea, eb = jnp.exp2(la - high), jnp.exp2(lb - high)
        total = ea + eb
        store_lse(o_ref, n, high + jnp.log2(total))
        ea, eb = ea / total, eb / total
        for k in range(4):
            span = pl.ds(k * 128, 128)
            mixed = column(ea[k : k + 1]) * a_ref[n, span, :].astype(F32)
            mixed = mixed + column(eb[k : k + 1]) * b_ref[n, span, :].astype(F32)
            o_ref[n, span, :] = mixed.astype(BF)


def merge_two(a, b):
    return ones_call(merge_two_body, jax.ShapeDtypeStruct(a.shape, BF), 8, "merge_two")(a, b)


def merge_body(part_ref, o_ref):
    count = part_ref.shape[0]
    lses = [load_lse(part_ref, s) for s in range(count)]
    high = functools.reduce(jnp.maximum, lses)
    shares = [jnp.exp2(v - high) for v in lses]
    total = functools.reduce(jnp.add, shares)
    shares = [v / total for v in shares]
    for k in range(4):
        acc = jnp.zeros((128, HD), F32)
        for s in range(count):
            part = part_ref[s, pl.ds(k * 128, 128), :].astype(F32)
            acc = acc + column(shares[s][k : k + 1]) * part
        acc = acc.astype(BF)
        for n in range(4):
            o_ref[k * 4 + n] = acc[n // 2 * 64 : n // 2 * 64 + 64]


def merge(parts):
    return ones_call(merge_body, jax.ShapeDtypeStruct((N, 64, HD), BF), 8, "merge")(parts)


def bf16_terms(v):
    hi = v.astype(BF).astype(F32)
    mid = (v - hi).astype(BF).astype(F32)
    return [hi, mid, v - hi - mid]


def project_body(
    pos_ref, att_ref, wa_ref, wb_ref, scale_ref, shift_ref, fw_ref, fb_ref, *refs
):
    own_ref, send_ref, const_ref, rows, x, stats = refs
    step = pl.program_id(0)
    core, side = pos_ref[0], pos_ref[1]
    cols = wa_ref.shape[1]
    half = D // 2
    contract = (((1,), (1,)), ((), ()))

    @pl.when(step == 0)
    def _():
        for h in range(HEADS):
            rows[:, h * HD : (h + 1) * HD] = att_ref[h]
        moved = jnp.zeros((1, 128), F32)
        blank = jnp.zeros((64, half), BF)
        for s in range(2):
            span = pl.ds(s * half, half)
            terms = bf16_terms(1.0 + scale_ref[:, span]) + bf16_terms(shift_ref[:, span])
            lhs = jnp.concatenate(terms + [jnp.zeros((2, half), F32)], axis=0).astype(BF)
            rhs = jnp.concatenate([fw_ref[:, span], blank], axis=0)
            got = lax.dot_general(lhs, rhs, contract, preferred_element_type=F32)
            const_ref[s : s + 1, :] = got[0:1] + got[1:2] + got[2:3]
            moved = moved + got[3:4] + got[4:5] + got[5:6]
        const_ref[2:3, :] = moved + fb_ref[...]

    a = rows[...]
    x[core, step] = jnp.dot(a, wa_ref[...], preferred_element_type=F32)
    x[1 - core, step] = jnp.dot(a, wb_ref[...], preferred_element_type=F32)

    @pl.when(step == pl.num_programs(0) - 1)
    def _():
        parts = [x[s, i] for s in range(2) for i in range(x.shape[1])]
        mean = sum(jnp.sum(p, axis=1, keepdims=True) for p in parts) * (1.0 / half)
        parts = [p - mean for p in parts]
        square = sum(jnp.sum(p * p, axis=1, keepdims=True) for p in parts)
        acc = jnp.zeros(stats.shape, F32)
        blank = jnp.zeros((64, cols), BF)
        for n, p in enumerate(parts):
            span = pl.ds(pl.multiple_of(side * half, 128) + n * cols, cols)
            m = (p * (1.0 + scale_ref[:, span])).astype(BF)
            rhs = jnp.concatenate([fw_ref[:, span], blank], axis=0)
            acc = acc + lax.dot_general(m, rhs, contract, preferred_element_type=F32)
        lane = lax.broadcasted_iota(jnp.int32, stats.shape, 1)
        stats[...] = jnp.where(lane < 64, acc, jnp.where(lane < 96, mean, square))
        own_ref[...] = stats[pl.ds(pl.multiple_of(side * 32, 32), 32), :]
        send_ref[...] = stats[pl.ds(pl.multiple_of(32 - side * 32, 32), 32), :]


def project(pos, att, wa, wb, scale, shift, fw, fb):
    cols = 384
    steps = wa.shape[1] // cols
    block = pl.BlockSpec((HEADS * HD, cols), lambda i: (0, i))

    def whole(shape):
        return pl.BlockSpec(shape, lambda i: (0,) * len(shape))

    count = att.shape[1]
    outs = [(32, 128), (32, 128), (8, 128)]
    return pl.pallas_call(
        project_body,
        grid=(steps,),
        in_specs=[
            pl.BlockSpec(memory_space=pltpu.SMEM),
            whole(att.shape),
            block,
            block,
            whole(scale.shape),
            whole(shift.shape),
            whole(fw.shape),
            whole(fb.shape),
        ],
        out_specs=[whole(o) for o in outs],
        out_shape=[jax.ShapeDtypeStruct(o, F32) for o in outs],
        scratch_shapes=[
            pltpu.VMEM((count, HEADS * HD), BF),
            pltpu.VMEM((2, steps, count, cols), F32),
            pltpu.VMEM((count, 128), F32),
        ],
        compiler_params=pltpu.CompilerParams(vmem_limit_bytes=12 * MIB),
        name="project",
    )(pos, att, wa, wb, scale, shift, fw, fb)


def finish_body(pos_ref, own_ref, got_ref, const_ref, upper_ref, lower_ref):
    side = pos_ref[1]
    own, got = own_ref[...], got_ref[...]
    m_own, m_got = own[:, 64:65], got[:, 64:65]
    apart = m_own - m_got
    square = own[:, 96:97] + got[:, 96:97] + apart * apart * (D / 4)
    rstd = lax.rsqrt(square * (1.0 / D) + NORM_EPS)
    first, second = const_ref[0:1, :], const_ref[1:2, :]
    u_own = jnp.where(side == 0, first, second)
    u_got = jnp.where(side == 0, second, first)
    total = own + got + (0.5 * apart) * (u_own - u_got)
    out = (total * rstd + const_ref[2:3, :]).astype(BF)[:, :64]

    src = lax.broadcasted_iota(jnp.int32, (64, 128), 0)
    dst = lax.broadcasted_iota(jnp.int32, (64, 128), 1)
    place = (src % 2) * 32 + (src // 2 % 2) * 16 + src // 4
    to = lax.broadcasted_iota(jnp.int32, (16, 32), 0)
    row = lax.broadcasted_iota(jnp.int32, (16, 32), 1)
    acc = jnp.zeros((16, 128), F32)
    for j in range(2):
        perm = jnp.where(dst == place + 64 * j, 1.0, 0.0).astype(BF)
        pick = jnp.where(row == (to % 8 * 2 + to // 8) * 2 + j, 1.0, 0.0).astype(BF)
        lanes = jnp.dot(out, perm, preferred_element_type=F32).astype(BF)
        acc = acc + jnp.dot(pick, lanes, preferred_element_type=F32)
    upper_ref[...] = acc[:8].astype(BF)
    lower_ref[...] = acc[8:].astype(BF)


def finish(pos, own, got, const):
    vmem = pl.BlockSpec(memory_space=pltpu.VMEM)
    return pl.pallas_call(
        finish_body,
        in_specs=[pl.BlockSpec(memory_space=pltpu.SMEM), vmem, vmem, vmem],
        out_shape=[jax.ShapeDtypeStruct((8, 128), BF)] * 2,
        compiler_params=pltpu.CompilerParams(vmem_limit_bytes=2 * MIB),
        name="finish",
    )(pos, own, got, const)


def spread_body(*refs):
    o_ref = refs[-1]
    rows = jnp.concatenate([ref[...].astype(F32) for ref in refs[:-1]], axis=0).astype(BF)
    o_ref[...] = jnp.broadcast_to(rows[None], o_ref.shape)


def spread(*rows):
    return ones_call(spread_body, jax.ShapeDtypeStruct((N, 32, 128), BF), 2, "spread")(*rows)


def conv_body(blk_ref, r_ref, k1_ref, b1_ref, k2_ref, b2_ref, o_ref, win, feat, w1, w2):
    blank = jnp.zeros((16, CH), BF)
    for a in range(3):
        for wr in range(4):
            for wc in range(4):
                ry, p = divmod(wr, 2)
                row = ((a * 2 + ry) * 4 + wc) * 32 + p * 16
                for ey in range(2):
                    for ex in range(2):
                        b, g = wr - ey, wc - ex
                        hit = 0 <= b < 3 and 0 <= g < 3
                        tile = k1_ref[(a * 3 + b) * 3 + g] if hit else blank
                        w1[pl.ds(row, 16), pl.ds((ey * 2 + ex) * CH, CH)] = tile
    taps = ((1, 0, None, 2), (2, 1, 0, None))
    blank = jnp.zeros((32, CH), BF)
    for a in range(3):
        for u, pair in enumerate(((2, None), (1, 2), (0, 1), (None, 0))):
            for ey, b in enumerate(pair):
                for qi in range(2):
                    for n, g in enumerate(taps[qi]):
                        hit = b is not None and g is not None
                        tile = k2_ref[(a * 3 + b) * 3 + g] if hit else blank
                        span = pl.ds((ey * 2 + qi) * CH, CH)
                        w2[a, pl.ds(u * 128 + n * 32, 32), span] = tile

    rows = r_ref[...].astype(F32).reshape(512, 128)
    lane = lax.broadcasted_iota(jnp.int32, (512, 128), 1)
    col = lax.broadcasted_iota(jnp.int32, (512, 128), 0) % 16
    before = jnp.where(col == 0, 0.0, pltpu.roll(rows, 1, 0))
    after = jnp.where(col == 15, 0.0, pltpu.roll(rows, 511, 0))
    views = (
        pltpu.roll(jnp.where(lane < 96, rows, before), 32, 1),
        pltpu.roll(jnp.where(lane < 32, after, rows), 96, 1),
    )
    for j, view in enumerate(views):
        view = view.astype(BF).reshape(4, 8, 16, 128)
        for r in range(3):
            for ry in range(2):
                span = pl.ds(ry * 128, 128)
                win[j, 2:, r, :, span] = view[r + ry]
                for early in range(2):
                    win[j, early, r, :, span] = view[r + ry, 0]

    top = jnp.where(blk_ref[0] == 0, 0.0, 1.0)
    bottom = jnp.where(blk_ref[0] == N - 1, 0.0, 1.0)
    for j in range(2):
        lhs = jnp.concatenate([win[j, a : a + 8] for a in range(3)], axis=-1)
        lhs = lhs.reshape(8 * 3 * 16, lhs.shape[-1])
        for n in range(4):
            span = pl.ds(n * CH, CH)
            v = jnp.dot(lhs, w1[:, span], preferred_element_type=F32) + b1_ref[...]
            v = (v / (1.0 + jnp.exp(-v))).reshape(8, 3, 16, CH)
            for r in range(3):
                f = v[:, r]
                if (r, n // 2) == (0, 0):
                    f = f * top
                if (r, n // 2) == (2, 1):
                    f = f * bottom
                f = f.astype(BF)
                feat[j, 2:, r, :, span] = f
                feat[j, 0, r, :, span] = f[0]
                feat[j, 1, r, :, span] = f[0]

    def product(a, r, first):
        lhs = feat[:, a : a + 8, r].reshape(256, 4 * CH)
        rhs = w2[a, pl.ds(first, 256), :]
        return lax.dot_general(lhs, rhs, (((1,), (1,)), ((), ())), preferred_element_type=F32)

    lane = lax.broadcasted_iota(jnp.int32, (128, 128), 1)
    col = lax.broadcasted_iota(jnp.int32, (128, 128), 0) % 16
    for pair in range(2):
        acc = jnp.zeros((256, 256), F32)
        for a in range(3):
            acc = acc + product(a, pair, 256) + product(a, pair + 1, 0)
        for y in range(2):
            z = acc[:, y * 128 : (y + 1) * 128]
            z0, z1 = z[:128], z[128:]
            right = jnp.where(col == 0, 0.0, pltpu.roll(z1, 1, 0))
            left = jnp.where(col == 15, 0.0, pltpu.roll(z0, 127, 0))
            s0 = z0 + pltpu.roll(jnp.where(lane < 96, right, z1), 64, 1)
            s1 = z1 + pltpu.roll(jnp.where(lane < 96, z0, left), 64, 1)
            out = jnp.where(lane < 64, s0, pltpu.roll(s1, 64, 1)) + b2_ref[...]
            o_ref[pair * 2 + y] = out.astype(BF).reshape(8, 16, 128)


def conv_stage(blk, rows, k1, b1, k2, b2):
    vmem = pl.BlockSpec(memory_space=pltpu.VMEM)
    return pl.pallas_call(
        conv_body,
        in_specs=[pl.BlockSpec(memory_space=pltpu.SMEM)] + [vmem] * 5,
        out_shape=jax.ShapeDtypeStruct((4, 8, 16, 128), BF),
        scratch_shapes=[
            pltpu.VMEM((2, 10, 3, 16, 256), BF),
            pltpu.VMEM((2, 10, 3, 16, 4 * CH), BF),
            pltpu.VMEM((768, 4 * CH), BF),
            pltpu.VMEM((3, 512, 4 * CH), BF),
        ],
        compiler_params=pltpu.CompilerParams(vmem_limit_bytes=24 * MIB),
        name="convs",
    )(blk, rows, k1, b1, k2, b2)


def after(value, *others):
    return lax.optimization_barrier((value,) + others)[0]


def shards(
    qkv,
    query_blocks,
    out_weight,
    mod_shift,
    mod_scale,
    final_weight,
    final_bias,
    conv_in_weight,
    conv_in_bias,
    conv_weight,
    conv_bias,
):
    head = lax.axis_index("head")
    blk = lax.axis_index("blk")
    core = blk % 2
    side = head % 2
    pos = jnp.stack([core, side])

    q_send = split_heads(qkv, (0,))
    kv_send = split_heads(qkv, (1, 2))
    q_all = lax.all_to_all(q_send, "head", 0, 0, tiled=True)
    kv_own = lax.all_to_all(after(kv_send, q_all), "head", 0, 0, tiled=True)
    kv_own = kv_own.reshape(-1, 2 * HD)

    near = select_queries(query_blocks, q_all)
    both = jnp.concatenate([near, lax.ppermute(near, "blk", FAR_SWAP)], axis=0)
    queries = [both]
    for m in range(1, 4):
        swap = [(i, i ^ (2 * m)) for i in range(N)]
        queries.append(lax.ppermute(both, "blk", swap))
    kv_own = after(kv_own, *queries)
    kv_other = lax.ppermute(kv_own, "blk", NEXT_SWAP)

    quarter = D // 4
    mine, theirs = (side * 2 + core) * quarter, ((1 - side) * 2 + core) * quarter
    source = after(out_weight, q_send)
    part = lax.dynamic_slice_in_dim(source, mine, quarter, axis=1)
    given = lax.dynamic_slice_in_dim(source, theirs, quarter, axis=1)
    given = lax.ppermute(given, "head", NEXT_SWAP)
    pair = jnp.stack([jnp.where(side == 0, part, given), jnp.where(side == 0, given, part)])
    pair = after(pair, kv_own)
    weight_a = lax.all_gather(pair, "head", axis=0, tiled=True, axis_index_groups=GROUPS_Z)

    place = (blk // 2 % 4).reshape(1)
    far_part = attention(1, place, queries, kv_own, kv_other)
    got_part = lax.ppermute(far_part, "blk", FAR_SWAP)
    near_part = attention(0, after(place, far_part), queries, kv_own, kv_other)
    partial = merge_two(near_part, got_part)

    partial = lax.all_to_all(partial, "blk", 0, 0, tiled=True, axis_index_groups=GROUPS_Y)

    attended = merge(partial)

    weight_a = after(weight_a, attended).reshape(HEADS * HD, quarter)
    weight_b = lax.ppermute(weight_a, "blk", NEXT_SWAP)

    attended = lax.all_to_all(attended, "head", 0, 0, tiled=True)
    own, send, const = project(
        pos,
        attended,
        weight_a,
        weight_b,
        mod_scale.reshape(1, D),
        mod_shift.reshape(1, D),
        jnp.transpose(final_weight),
        jnp.pad(final_bias, (0, 64)).reshape(1, 128),
    )
    upper, lower = finish(pos, own, lax.ppermute(send, "head", NEXT_SWAP), const)

    ends = N - 1
    above = lax.ppermute(lower, "blk", [(i, i + 1) for i in range(ends)])
    below = lax.ppermute(upper, "blk", [(i + 1, i) for i in range(ends)])
    rows = lax.all_to_all(spread(above, upper, lower, below), "head", 0, 0, tiled=True)
    bias_out = lax.dynamic_slice_in_dim(conv_bias, head * 32, 32)
    out = conv_stage(
        blk.reshape(1),
        jnp.transpose(rows, (1, 0, 2)),
        conv_in_weight.reshape(27, 16, CH),
        conv_in_bias.reshape(1, CH),
        jnp.transpose(conv_weight, (0, 1, 2, 4, 3)).reshape(27, 32, CH),
        jnp.tile(bias_out, 4).reshape(1, -1),
    )
    out = lax.all_to_all(jnp.transpose(out, (2, 0, 1, 3)), "head", 0, 0, tiled=True)
    out = jnp.transpose(out.reshape(N, 4, 8, 4, 32), (2, 1, 3, 0, 4))
    return out.reshape(8, 4, 4, CH)


def solution(mesh):
    in_specs = (
        P("blk", "head", None),
        P("blk"),
        P("head", None),
        P(),
        P(),
        P(),
        P(),
        P(),
        P(),
        P(None, None, None, None, "head"),
        P(),
    )
    out_specs = P(None, "blk", "head", None)
    return jax.shard_map(shards, mesh=mesh, in_specs=in_specs, out_specs=out_specs, check_vma=False)
```

```python
import functools
import math

import jax
import jax.numpy as jnp
from jax import lax
from jax.experimental import pallas as pl
from jax.experimental.pallas import tpu as pltpu
from jax.sharding import PartitionSpec as P

HEADS = 16
HD = 128
D = 3072
QBLK = 128
QROWS = 512
CH = 512
NORM_EPS = 1e-06
BF = jnp.bfloat16
F32 = jnp.float32
COEF = math.log2(math.e) / math.sqrt(HD)
MIB = 2**20

N = 16
GROUPS_Z = [[x + 2 * k for k in range(8)] for x in range(2)]
NEXT_SWAP = [(i, i ^ 1) for i in range(N)]
Y_SWAPS = [[(i, i ^ (2 * m)) for i in range(N)] for m in range(4)]
FAR_SWAP = [(i, i ^ 8) for i in range(N)]


def ones_call(body, out_shape, limit, name):
    return pl.pallas_call(
        body,
        out_shape=out_shape,
        compiler_params=pltpu.CompilerParams(vmem_limit_bytes=limit * MIB),
        name=name,
    )


def split_body(*refs):
    o_ref = refs[-1]
    for n, ref in enumerate(refs[:-1]):
        for h in range(HEADS):
            o_ref[h, :, n * HD : (n + 1) * HD] = ref[0, :, h * HD : (h + 1) * HD]


def split_heads(qkv, parts):
    tok = qkv.shape[1]
    return pl.pallas_call(
        split_body,
        grid=(1,),
        in_specs=[
            pl.BlockSpec((1, tok, HEADS * HD), lambda i, p=p: (0, 0, p)) for p in parts
        ],
        out_specs=pl.BlockSpec((HEADS, tok, len(parts) * HD), lambda i: (0, 0, 0)),
        out_shape=jax.ShapeDtypeStruct((HEADS, tok, len(parts) * HD), BF),
        compiler_params=pltpu.CompilerParams(vmem_limit_bytes=56 * MIB),
        name="split",
    )(*[qkv] * len(parts))


def select_body(chosen_ref, q_ref, o_ref):
    for i in range(QROWS // QBLK):
        o_ref[pl.ds(i * QBLK, QBLK), :] = q_ref[chosen_ref[i] % N]


def select_queries(chosen, q_all):
    return pl.pallas_call(
        select_body,
        in_specs=[
            pl.BlockSpec(memory_space=pltpu.SMEM),
            pl.BlockSpec(memory_space=pltpu.VMEM),
        ],
        out_shape=jax.ShapeDtypeStruct((QROWS, HD), BF),
        compiler_params=pltpu.CompilerParams(vmem_limit_bytes=4 * MIB),
        name="select",
    )(chosen, q_all)


def pack_body(own_ref, other_ref, keys, vals):
    half = own_ref.shape[0]
    for s, ref in enumerate((own_ref, other_ref)):
        rows = pl.ds(s * half, half)
        keys[rows, :HD] = ref[:, :HD]
        keys[rows, HD:] = ref[:, :HD]
        vals[rows, :HD] = ref[:, HD:]
        vals[rows, HD:] = jnp.ones((half, HD), BF)


def pack(own, other):
    shape = jax.ShapeDtypeStruct((2 * own.shape[0], 2 * HD), BF)
    return ones_call(pack_body, [shape, shape], 8, "pack")(own, other)


def store_lse(o_ref, chunk, lse):
    hi = lse.astype(BF).astype(F32)
    mid = (lse - hi).astype(BF).astype(F32)
    low = lse - hi - mid
    tail = jnp.concatenate([hi, mid, low, jnp.zeros_like(hi)], axis=0)
    o_ref[chunk, QROWS:, :] = tail.astype(BF)


def load_lse(ref, s):
    tail = ref[s, QROWS:, :].astype(F32)
    return tail[0:4] + tail[4:8] + tail[8:12]


def column(row):
    return jnp.transpose(jnp.broadcast_to(row, (128, 128)))


def attention_body(sub, q_ref, keys, vals, o_ref):
    def scores(chunk, first):
        q = q_ref[pl.ds(chunk * QROWS + first, sub), :].astype(F32) * COEF
        hi = q.astype(BF)
        lo = (q - hi.astype(F32)).astype(BF)
        return lax.dot_general(
            jnp.concatenate([hi, lo], axis=1),
            keys[...],
            (((1,), (1,)), ((), ())),
            preferred_element_type=F32,
        )

    tiles = [(chunk, first) for chunk in range(2) for first in range(0, QROWS, sub)]
    lse_rows = []
    current = scores(*tiles[0])
    for n, (chunk, first) in enumerate(tiles):
        later = scores(*tiles[n + 1]) if n + 1 < len(tiles) else None
        high = jnp.max(current, axis=1, keepdims=True)
        weights = jnp.exp2(current - high).astype(BF)
        acc = jnp.dot(weights, vals[...], preferred_element_type=F32)
        total = acc[:, HD:]
        o_ref[chunk, first : first + sub, :] = (acc[:, :HD] / total).astype(BF)
        lse = high + jnp.log2(total)
        for k in range(sub // 128):
            lse_rows.append(jnp.transpose(lse[k * 128 : (k + 1) * 128])[:1])
        if first + sub == QROWS:
            store_lse(o_ref, chunk, jnp.concatenate(lse_rows, axis=0))
            lse_rows = []
        current = later


def attention(queries, keys, vals):
    count = keys.shape[0]
    return pl.pallas_call(
        functools.partial(attention_body, 256),
        in_specs=[pl.BlockSpec(memory_space=pltpu.VMEM)] * 3,
        out_shape=jax.ShapeDtypeStruct((2, QROWS + 16, HD), BF),
        compiler_params=pltpu.CompilerParams(vmem_limit_bytes=24 * MIB),
        cost_estimate=pl.CostEstimate(
            flops=12 * 2 * QROWS * count * 2 * HD,
            bytes_accessed=4 * MIB,
            transcendentals=2 * QROWS * count,
        ),
        name="attention",
    )(queries, keys, vals)


def merged(refs, n):
    lses = [load_lse(ref, n) for ref in refs]
    high = functools.reduce(jnp.maximum, lses)
    shares = [jnp.exp2(v - high) for v in lses]
    total = functools.reduce(jnp.add, shares)
    shares = [v / total for v in shares]
    blocks = []
    for k in range(4):
        acc = jnp.zeros((128, HD), F32)
        for share, ref in zip(shares, refs):
            part = ref[n, pl.ds(k * 128, 128), :].astype(F32)
            acc = acc + column(share[k : k + 1]) * part
        blocks.append(acc.astype(BF))
    return blocks, high + jnp.log2(total)


def merge_body(n, *refs):
    o_ref = refs[-1]
    blocks, lse = merged(refs[:-1], n)
    for k, block in enumerate(blocks):
        o_ref[0, pl.ds(k * 128, 128), :] = block
    store_lse(o_ref, 0, lse)


def merge(n, parts):
    shape = jax.ShapeDtypeStruct((1, QROWS + 16, HD), BF)
    return ones_call(functools.partial(merge_body, n), shape, 8, "merge")(*parts)


def merge_last_body(a_ref, b_ref, o_ref):
    blocks, _ = merged((a_ref, b_ref), 0)
    for k, block in enumerate(blocks):
        for n in range(4):
            o_ref[k * 4 + n] = block[n // 2 * 64 : n // 2 * 64 + 64]


def merge_last(a, b):
    shape = jax.ShapeDtypeStruct((N, 64, HD), BF)
    return ones_call(merge_last_body, shape, 8, "merge_last")(a, b)


def bf16_terms(v):
    hi = v.astype(BF).astype(F32)
    mid = (v - hi).astype(BF).astype(F32)
    return [hi, mid, v - hi - mid]


def project_body(
    pos_ref, att_ref, wa_ref, wb_ref, scale_ref, shift_ref, fw_ref, fb_ref, *refs
):
    own_ref, send_ref, const_ref, rows, x, stats = refs
    core, side = pos_ref[0], pos_ref[1]
    cols = wa_ref.shape[1]
    half = D // 2
    contract = (((1,), (1,)), ((), ()))
    for h in range(HEADS):
        rows[:, h * HD : (h + 1) * HD] = att_ref[h ^ side]
    a = rows[...]
    x[core] = jnp.dot(a, wa_ref[...], preferred_element_type=F32)
    x[1 - core] = jnp.dot(a, wb_ref[...], preferred_element_type=F32)

    moved = jnp.zeros((1, 128), F32)
    blank = jnp.zeros((64, half), BF)
    for s in range(2):
        span = pl.ds(s * half, half)
        terms = bf16_terms(1.0 + scale_ref[:, span]) + bf16_terms(shift_ref[:, span])
        lhs = jnp.concatenate(terms + [jnp.zeros((2, half), F32)], axis=0).astype(BF)
        rhs = jnp.concatenate([fw_ref[:, span], blank], axis=0)
        got = lax.dot_general(lhs, rhs, contract, preferred_element_type=F32)
        const_ref[s : s + 1, :] = got[0:1] + got[1:2] + got[2:3]
        moved = moved + got[3:4] + got[4:5] + got[5:6]
    const_ref[2:3, :] = moved + fb_ref[...]

    parts = [x[0], x[1]]
    mean = sum(jnp.sum(p, axis=1, keepdims=True) for p in parts) * (1.0 / half)
    parts = [p - mean for p in parts]
    square = sum(jnp.sum(p * p, axis=1, keepdims=True) for p in parts)
    acc = jnp.zeros(stats.shape, F32)
    blank = jnp.zeros((64, cols), BF)
    for n, p in enumerate(parts):
        span = pl.ds(pl.multiple_of(side * half, 128) + n * cols, cols)
        m = (p * (1.0 + scale_ref[:, span])).astype(BF)
        rhs = jnp.concatenate([fw_ref[:, span], blank], axis=0)
        acc = acc + lax.dot_general(m, rhs, contract, preferred_element_type=F32)
    lane = lax.broadcasted_iota(jnp.int32, stats.shape, 1)
    stats[...] = jnp.where(lane < 64, acc, jnp.where(lane < 96, mean, square))
    own_ref[...] = stats[pl.ds(pl.multiple_of(side * 32, 32), 32), :]
    send_ref[...] = stats[pl.ds(pl.multiple_of(32 - side * 32, 32), 32), :]


def project(pos, att, wa, wb, scale, shift, fw, fb):
    count, cols = att.shape[1], wa.shape[1]
    vmem = pl.BlockSpec(memory_space=pltpu.VMEM)
    return pl.pallas_call(
        project_body,
        in_specs=[pl.BlockSpec(memory_space=pltpu.SMEM)] + [vmem] * 7,
        out_shape=[jax.ShapeDtypeStruct(o, F32) for o in ((32, 128), (32, 128), (8, 128))],
        scratch_shapes=[
            pltpu.VMEM((count, HEADS * HD), BF),
            pltpu.VMEM((2, count, cols), F32),
            pltpu.VMEM((count, 128), F32),
        ],
        compiler_params=pltpu.CompilerParams(vmem_limit_bytes=12 * MIB),
        name="project",
    )(pos, att, wa, wb, scale, shift, fw, fb)


def finish_body(pos_ref, own_ref, got_ref, const_ref, upper_ref, lower_ref):
    side = pos_ref[1]
    own, got = own_ref[...], got_ref[...]
    m_own, m_got = own[:, 64:65], got[:, 64:65]
    apart = m_own - m_got
    square = own[:, 96:97] + got[:, 96:97] + apart * apart * (D / 4)
    rstd = lax.rsqrt(square * (1.0 / D) + NORM_EPS)
    first, second = const_ref[0:1, :], const_ref[1:2, :]
    u_own = jnp.where(side == 0, first, second)
    u_got = jnp.where(side == 0, second, first)
    total = own + got + (0.5 * apart) * (u_own - u_got)
    out = (total * rstd + const_ref[2:3, :]).astype(BF)[:, :64]

    src = lax.broadcasted_iota(jnp.int32, (64, 128), 0)
    dst = lax.broadcasted_iota(jnp.int32, (64, 128), 1)
    place = (src % 2) * 32 + (src // 2 % 2) * 16 + src // 4
    to = lax.broadcasted_iota(jnp.int32, (16, 32), 0)
    row = lax.broadcasted_iota(jnp.int32, (16, 32), 1)
    acc = jnp.zeros((16, 128), F32)
    for j in range(2):
        perm = jnp.where(dst == place + 64 * j, 1.0, 0.0).astype(BF)
        pick = jnp.where(row == (to % 8 * 2 + to // 8) * 2 + j, 1.0, 0.0).astype(BF)
        lanes = jnp.dot(out, perm, preferred_element_type=F32).astype(BF)
        acc = acc + jnp.dot(pick, lanes, preferred_element_type=F32)
    upper_ref[...] = acc[:8].astype(BF)
    lower_ref[...] = acc[8:].astype(BF)


def finish(pos, own, got, const):
    vmem = pl.BlockSpec(memory_space=pltpu.VMEM)
    return pl.pallas_call(
        finish_body,
        in_specs=[pl.BlockSpec(memory_space=pltpu.SMEM), vmem, vmem, vmem],
        out_shape=[jax.ShapeDtypeStruct((8, 128), BF)] * 2,
        compiler_params=pltpu.CompilerParams(vmem_limit_bytes=2 * MIB),
        name="finish",
    )(pos, own, got, const)


def spread_body(*refs):
    o_ref = refs[-1]
    rows = jnp.concatenate([ref[...].astype(F32) for ref in refs[:-1]], axis=0).astype(BF)
    o_ref[...] = jnp.broadcast_to(rows[None], o_ref.shape)


def spread(*rows):
    return ones_call(spread_body, jax.ShapeDtypeStruct((N, 32, 128), BF), 2, "spread")(*rows)


def conv_body(blk_ref, r_ref, k1_ref, b1_ref, k2_ref, b2_ref, o_ref, win, feat, w1, w2):
    blank = jnp.zeros((16, CH), BF)
    for a in range(3):
        for wr in range(4):
            for wc in range(4):
                ry, p = divmod(wr, 2)
                row = ((a * 2 + ry) * 4 + wc) * 32 + p * 16
                for ey in range(2):
                    for ex in range(2):
                        b, g = wr - ey, wc - ex
                        hit = 0 <= b < 3 and 0 <= g < 3
                        tile = k1_ref[(a * 3 + b) * 3 + g] if hit else blank
                        w1[pl.ds(row, 16), pl.ds((ey * 2 + ex) * CH, CH)] = tile
    taps = ((1, 0, None, 2), (2, 1, 0, None))
    blank = jnp.zeros((32, CH), BF)
    for a in range(3):
        for u, pair in enumerate(((2, None), (1, 2), (0, 1), (None, 0))):
            for ey, b in enumerate(pair):
                for qi in range(2):
                    for n, g in enumerate(taps[qi]):
                        hit = b is not None and g is not None
                        tile = k2_ref[(a * 3 + b) * 3 + g] if hit else blank
                        span = pl.ds((ey * 2 + qi) * CH, CH)
                        w2[a, pl.ds(u * 128 + n * 32, 32), span] = tile

    rows = r_ref[...].astype(F32).reshape(512, 128)
    lane = lax.broadcasted_iota(jnp.int32, (512, 128), 1)
    col = lax.broadcasted_iota(jnp.int32, (512, 128), 0) % 16
    before = jnp.where(col == 0, 0.0, pltpu.roll(rows, 1, 0))
    after = jnp.where(col == 15, 0.0, pltpu.roll(rows, 511, 0))
    views = (
        pltpu.roll(jnp.where(lane < 96, rows, before), 32, 1),
        pltpu.roll(jnp.where(lane < 32, after, rows), 96, 1),
    )
    for j, view in enumerate(views):
        view = view.astype(BF).reshape(4, 8, 16, 128)
        for r in range(3):
            for ry in range(2):
                span = pl.ds(ry * 128, 128)
                win[j, 2:, r, :, span] = view[r + ry]
                for early in range(2):
                    win[j, early, r, :, span] = view[r + ry, 0]

    top = jnp.where(blk_ref[0] == 0, 0.0, 1.0)
    bottom = jnp.where(blk_ref[0] == N - 1, 0.0, 1.0)
    for j in range(2):
        lhs = jnp.concatenate([win[j, a : a + 8] for a in range(3)], axis=-1)
        lhs = lhs.reshape(8 * 3 * 16, lhs.shape[-1])
        for n in range(4):
            span = pl.ds(n * CH, CH)
            v = jnp.dot(lhs, w1[:, span], preferred_element_type=F32) + b1_ref[...]
            v = (v / (1.0 + jnp.exp(-v))).reshape(8, 3, 16, CH)
            for r in range(3):
                f = v[:, r]
                if (r, n // 2) == (0, 0):
                    f = f * top
                if (r, n // 2) == (2, 1):
                    f = f * bottom
                f = f.astype(BF)
                feat[j, 2:, r, :, span] = f
                feat[j, 0, r, :, span] = f[0]
                feat[j, 1, r, :, span] = f[0]

    def product(a, r, first):
        lhs = feat[:, a : a + 8, r].reshape(256, 4 * CH)
        rhs = w2[a, pl.ds(first, 256), :]
        return lax.dot_general(lhs, rhs, (((1,), (1,)), ((), ())), preferred_element_type=F32)

    lane = lax.broadcasted_iota(jnp.int32, (128, 128), 1)
    col = lax.broadcasted_iota(jnp.int32, (128, 128), 0) % 16
    for pair in range(2):
        acc = jnp.zeros((256, 256), F32)
        for a in range(3):
            acc = acc + product(a, pair, 256) + product(a, pair + 1, 0)
        for y in range(2):
            z = acc[:, y * 128 : (y + 1) * 128]
            z0, z1 = z[:128], z[128:]
            right = jnp.where(col == 0, 0.0, pltpu.roll(z1, 1, 0))
            left = jnp.where(col == 15, 0.0, pltpu.roll(z0, 127, 0))
            s0 = z0 + pltpu.roll(jnp.where(lane < 96, right, z1), 64, 1)
            s1 = z1 + pltpu.roll(jnp.where(lane < 96, z0, left), 64, 1)
            out = jnp.where(lane < 64, s0, pltpu.roll(s1, 64, 1)) + b2_ref[...]
            o_ref[pair * 2 + y] = out.astype(BF).reshape(8, 16, 128)


def conv_stage(blk, rows, k1, b1, k2, b2):
    vmem = pl.BlockSpec(memory_space=pltpu.VMEM)
    return pl.pallas_call(
        conv_body,
        in_specs=[pl.BlockSpec(memory_space=pltpu.SMEM)] + [vmem] * 5,
        out_shape=jax.ShapeDtypeStruct((4, 8, 16, 128), BF),
        scratch_shapes=[
            pltpu.VMEM((2, 10, 3, 16, 256), BF),
            pltpu.VMEM((2, 10, 3, 16, 4 * CH), BF),
            pltpu.VMEM((768, 4 * CH), BF),
            pltpu.VMEM((3, 512, 4 * CH), BF),
        ],
        compiler_params=pltpu.CompilerParams(vmem_limit_bytes=24 * MIB),
        name="convs",
    )(blk, rows, k1, b1, k2, b2)


def after(value, *others):
    return lax.optimization_barrier((value,) + others)[0]


def shards(
    qkv,
    query_blocks,
    out_weight,
    mod_shift,
    mod_scale,
    final_weight,
    final_bias,
    conv_in_weight,
    conv_in_bias,
    conv_weight,
    conv_bias,
):
    head = lax.axis_index("head")
    blk = lax.axis_index("blk")
    core = blk % 2
    side = head % 2
    pos = jnp.stack([core, side])

    q_send = split_heads(qkv, (0,))
    quarter = D // 4
    mine, theirs = (side * 2 + core) * quarter, ((1 - side) * 2 + core) * quarter
    source = after(out_weight, q_send)
    part = lax.dynamic_slice_in_dim(source, mine, quarter, axis=1)
    given = lax.dynamic_slice_in_dim(source, theirs, quarter, axis=1)
    pair = jnp.stack([part, lax.ppermute(given, "head", NEXT_SWAP)])

    q_all = lax.all_to_all(q_send, "head", 0, 0, tiled=True)
    kv_send = after(split_heads(qkv, (1, 2)), q_all, pair)
    kv_got = lax.all_to_all(kv_send, "head", 0, 0, tiled=True).reshape(-1, 2 * HD)
    weight_a = lax.all_gather(
        after(pair, kv_got), "head", axis=0, tiled=True, axis_index_groups=GROUPS_Z
    )

    near = select_queries(query_blocks, q_all)
    both = jnp.concatenate([near, lax.ppermute(near, "blk", FAR_SWAP)], axis=0)
    queries = [both]
    for m in range(1, 4):
        queries.append(lax.ppermute(both, "blk", Y_SWAPS[m]))
    kv_own = after(kv_got, *queries)
    kv_other = lax.ppermute(kv_own, "blk", NEXT_SWAP)

    keys, vals = pack(kv_own, kv_other)
    part_2 = attention(queries[2], keys, vals)
    got_2 = lax.ppermute(part_2, "blk", Y_SWAPS[2])
    part_1 = attention(after(queries[1], part_2), keys, vals)
    got_1 = lax.ppermute(part_1, "blk", Y_SWAPS[1])
    part_3 = attention(after(queries[3], part_1, got_2), keys, vals)
    got_3 = lax.ppermute(part_3, "blk", Y_SWAPS[3])
    part_0 = attention(after(queries[0], part_3, got_1), keys, vals)
    parts = (part_0, got_1, got_2, got_3)
    attended = merge_last(merge(0, parts), lax.ppermute(merge(1, parts), "blk", FAR_SWAP))

    weight_a = after(weight_a, attended).reshape(HEADS * HD, quarter)
    weight_b = lax.ppermute(weight_a, "blk", NEXT_SWAP)

    attended = lax.all_to_all(attended, "head", 0, 0, tiled=True)
    own, send, const = project(
        pos,
        attended,
        weight_a,
        weight_b,
        mod_scale.reshape(1, D),
        mod_shift.reshape(1, D),
        jnp.transpose(final_weight),
        jnp.pad(final_bias, (0, 64)).reshape(1, 128),
    )
    upper, lower = finish(pos, own, lax.ppermute(send, "head", NEXT_SWAP), const)

    ends = N - 1
    above = lax.ppermute(lower, "blk", [(i, i + 1) for i in range(ends)])
    below = lax.ppermute(upper, "blk", [(i + 1, i) for i in range(ends)])
    rows = lax.all_to_all(spread(above, upper, lower, below), "head", 0, 0, tiled=True)
    bias_out = lax.dynamic_slice_in_dim(conv_bias, head * 32, 32)
    out = conv_stage(
        blk.reshape(1),
        jnp.transpose(rows, (1, 0, 2)),
        conv_in_weight.reshape(27, 16, CH),
        conv_in_bias.reshape(1, CH),
        jnp.transpose(conv_weight, (0, 1, 2, 4, 3)).reshape(27, 32, CH),
        jnp.tile(bias_out, 4).reshape(1, -1),
    )
    out = lax.all_to_all(jnp.transpose(out, (2, 0, 1, 3)), "head", 0, 0, tiled=True)
    out = jnp.transpose(out.reshape(N, 4, 8, 4, 32), (2, 1, 3, 0, 4))
    return out.reshape(8, 4, 4, CH)


def solution(mesh):
    in_specs = (
        P("blk", "head", None),
        P("blk"),
        P("head", None),
        P(),
        P(),
        P(),
        P(),
        P(),
        P(),
        P(None, None, None, None, "head"),
        P(),
    )
    out_specs = P(None, "blk", "head", None)
    return jax.shard_map(shards, mesh=mesh, in_specs=in_specs, out_specs=out_specs, check_vma=False)
```

```python
import functools
import math

import jax
import jax.numpy as jnp
from jax import lax
from jax.experimental import pallas as pl
from jax.experimental.pallas import tpu as pltpu
from jax.sharding import PartitionSpec as P

HEADS = 16
HD = 128
D = 3072
QBLK = 128
QROWS = 512
CH = 512
NORM_EPS = 1e-06
BF = jnp.bfloat16
F32 = jnp.float32
COEF = math.log2(math.e) / math.sqrt(HD)
MIB = 2**20

N = 16
GROUPS_Z = [[x + 2 * k for k in range(8)] for x in range(2)]
NEXT_SWAP = [(i, i ^ 1) for i in range(N)]
Y_SWAPS = [[(i, i ^ (2 * m)) for i in range(N)] for m in range(4)]
FAR_SWAP = [(i, i ^ 8) for i in range(N)]


def ones_call(body, out_shape, limit, name):
    return pl.pallas_call(
        body,
        out_shape=out_shape,
        compiler_params=pltpu.CompilerParams(vmem_limit_bytes=limit * MIB),
        name=name,
    )


def split_body(*refs):
    o_ref = refs[-1]
    for n, ref in enumerate(refs[:-1]):
        for h in range(HEADS):
            o_ref[h, :, n * HD : (n + 1) * HD] = ref[0, :, h * HD : (h + 1) * HD]


def split_heads(qkv, parts):
    tok = qkv.shape[1]
    return pl.pallas_call(
        split_body,
        grid=(1,),
        in_specs=[
            pl.BlockSpec((1, tok, HEADS * HD), lambda i, p=p: (0, 0, p)) for p in parts
        ],
        out_specs=pl.BlockSpec((HEADS, tok, len(parts) * HD), lambda i: (0, 0, 0)),
        out_shape=jax.ShapeDtypeStruct((HEADS, tok, len(parts) * HD), BF),
        compiler_params=pltpu.CompilerParams(vmem_limit_bytes=56 * MIB),
        name="split",
    )(*[qkv] * len(parts))


def select_body(chosen_ref, q_ref, o_ref):
    for i in range(QROWS // QBLK):
        o_ref[pl.ds(i * QBLK, QBLK), :] = q_ref[chosen_ref[i] % N]


def select_queries(chosen, q_all):
    return pl.pallas_call(
        select_body,
        in_specs=[
            pl.BlockSpec(memory_space=pltpu.SMEM),
            pl.BlockSpec(memory_space=pltpu.VMEM),
        ],
        out_shape=jax.ShapeDtypeStruct((QROWS, HD), BF),
        compiler_params=pltpu.CompilerParams(vmem_limit_bytes=4 * MIB),
        name="select",
    )(chosen, q_all)


def pack_body(own_ref, other_ref, keys, vals):
    half = own_ref.shape[0]
    for s, ref in enumerate((own_ref, other_ref)):
        rows = pl.ds(s * half, half)
        keys[rows, :HD] = ref[:, :HD]
        keys[rows, HD:] = ref[:, :HD]
        vals[rows, :HD] = ref[:, HD:]
        vals[rows, HD:] = jnp.ones((half, HD), BF)


def pack(own, other):
    shape = jax.ShapeDtypeStruct((2 * own.shape[0], 2 * HD), BF)
    return ones_call(pack_body, [shape, shape], 8, "pack")(own, other)


def store_lse(o_ref, chunk, lse):
    hi = lse.astype(BF).astype(F32)
    mid = (lse - hi).astype(BF).astype(F32)
    low = lse - hi - mid
    tail = jnp.concatenate([hi, mid, low, jnp.zeros_like(hi)], axis=0)
    o_ref[chunk, QROWS:, :] = tail.astype(BF)


def load_lse(ref, s):
    tail = ref[s, QROWS:, :].astype(F32)
    return tail[0:4] + tail[4:8] + tail[8:12]


def column(row):
    return jnp.transpose(jnp.broadcast_to(row, (128, 128)))


def attention_body(sub, q_ref, keys, vals, o_ref):
    def scores(chunk, first):
        q = q_ref[pl.ds(chunk * QROWS + first, sub), :].astype(F32) * COEF
        hi = q.astype(BF)
        lo = (q - hi.astype(F32)).astype(BF)
        return lax.dot_general(
            jnp.concatenate([hi, lo], axis=1),
            keys[...],
            (((1,), (1,)), ((), ())),
            preferred_element_type=F32,
        )

    tiles = [(chunk, first) for chunk in range(2) for first in range(0, QROWS, sub)]
    lse_rows = []
    current = scores(*tiles[0])
    for n, (chunk, first) in enumerate(tiles):
        later = scores(*tiles[n + 1]) if n + 1 < len(tiles) else None
        high = jnp.max(current, axis=1, keepdims=True)
        weights = jnp.exp2(current - high).astype(BF)
        acc = jnp.dot(weights, vals[...], preferred_element_type=F32)
        total = acc[:, HD:]
        o_ref[chunk, first : first + sub, :] = (acc[:, :HD] / total).astype(BF)
        lse = high + jnp.log2(total)
        for k in range(sub // 128):
            lse_rows.append(jnp.transpose(lse[k * 128 : (k + 1) * 128])[:1])
        if first + sub == QROWS:
            store_lse(o_ref, chunk, jnp.concatenate(lse_rows, axis=0))
            lse_rows = []
        current = later


def attention(queries, keys, vals):
    count = keys.shape[0]
    return pl.pallas_call(
        functools.partial(attention_body, 256),
        in_specs=[pl.BlockSpec(memory_space=pltpu.VMEM)] * 3,
        out_shape=jax.ShapeDtypeStruct((2, QROWS + 16, HD), BF),
        compiler_params=pltpu.CompilerParams(vmem_limit_bytes=24 * MIB),
        cost_estimate=pl.CostEstimate(
            flops=12 * 2 * QROWS * count * 2 * HD,
            bytes_accessed=4 * MIB,
            transcendentals=2 * QROWS * count,
        ),
        name="attention",
    )(queries, keys, vals)


def merged(refs, n):
    lses = [load_lse(ref, n) for ref in refs]
    high = functools.reduce(jnp.maximum, lses)
    shares = [jnp.exp2(v - high) for v in lses]
    total = functools.reduce(jnp.add, shares)
    shares = [v / total for v in shares]
    blocks = []
    for k in range(4):
        acc = jnp.zeros((128, HD), F32)
        for share, ref in zip(shares, refs):
            part = ref[n, pl.ds(k * 128, 128), :].astype(F32)
            acc = acc + column(share[k : k + 1]) * part
        blocks.append(acc.astype(BF))
    return blocks, high + jnp.log2(total)


def merge_body(n, *refs):
    o_ref = refs[-1]
    blocks, lse = merged(refs[:-1], n)
    for k, block in enumerate(blocks):
        o_ref[0, pl.ds(k * 128, 128), :] = block
    store_lse(o_ref, 0, lse)


def merge(n, parts):
    shape = jax.ShapeDtypeStruct((1, QROWS + 16, HD), BF)
    return ones_call(functools.partial(merge_body, n), shape, 8, "merge")(*parts)


def merge_last_body(a_ref, b_ref, o_ref):
    blocks, _ = merged((a_ref, b_ref), 0)
    for k, block in enumerate(blocks):
        for n in range(4):
            o_ref[k * 4 + n] = block[n // 2 * 64 : n // 2 * 64 + 64]


def merge_last(a, b):
    shape = jax.ShapeDtypeStruct((N, 64, HD), BF)
    return ones_call(merge_last_body, shape, 8, "merge_last")(a, b)


def bf16_terms(v):
    hi = v.astype(BF).astype(F32)
    mid = (v - hi).astype(BF).astype(F32)
    return [hi, mid, v - hi - mid]


def project_body(
    blk_ref, head_ref, att_ref, wa_ref, wb_ref, scale_ref, shift_ref, fw_ref, fb_ref, *refs
):
    own_ref, send_ref, const_ref, rows, x, stats = refs
    core, side = blk_ref[0] % 2, head_ref[0] % 2
    cols = wa_ref.shape[1]
    half = D // 2
    contract = (((1,), (1,)), ((), ()))
    for h in range(HEADS):
        rows[:, h * HD : (h + 1) * HD] = att_ref[h ^ side]
    a = rows[...]
    x[core] = jnp.dot(a, wa_ref[...], preferred_element_type=F32)
    x[1 - core] = jnp.dot(a, wb_ref[...], preferred_element_type=F32)

    moved = jnp.zeros((1, 128), F32)
    blank = jnp.zeros((64, half), BF)
    for s in range(2):
        span = pl.ds(s * half, half)
        terms = bf16_terms(1.0 + scale_ref[:, span]) + bf16_terms(shift_ref[:, span])
        lhs = jnp.concatenate(terms + [jnp.zeros((2, half), F32)], axis=0).astype(BF)
        rhs = jnp.concatenate([fw_ref[:, span], blank], axis=0)
        got = lax.dot_general(lhs, rhs, contract, preferred_element_type=F32)
        const_ref[s : s + 1, :] = got[0:1] + got[1:2] + got[2:3]
        moved = moved + got[3:4] + got[4:5] + got[5:6]
    const_ref[2:3, :] = moved
    const_ref[2:3, :64] = moved[:, :64] + fb_ref[...]

    parts = [x[0], x[1]]
    mean = sum(jnp.sum(p, axis=1, keepdims=True) for p in parts) * (1.0 / half)
    parts = [p - mean for p in parts]
    square = sum(jnp.sum(p * p, axis=1, keepdims=True) for p in parts)
    acc = jnp.zeros(stats.shape, F32)
    blank = jnp.zeros((64, cols), BF)
    for n, p in enumerate(parts):
        span = pl.ds(pl.multiple_of(side * half, 128) + n * cols, cols)
        m = (p * (1.0 + scale_ref[:, span])).astype(BF)
        rhs = jnp.concatenate([fw_ref[:, span], blank], axis=0)
        acc = acc + lax.dot_general(m, rhs, contract, preferred_element_type=F32)
    lane = lax.broadcasted_iota(jnp.int32, stats.shape, 1)
    stats[...] = jnp.where(lane < 64, acc, jnp.where(lane < 96, mean, square))
    own_ref[...] = stats[pl.ds(pl.multiple_of(side * 32, 32), 32), :]
    send_ref[...] = stats[pl.ds(pl.multiple_of(32 - side * 32, 32), 32), :]


def project(blk, head, att, wa, wb, scale, shift, fw, fb):
    count, cols = att.shape[1], wa.shape[1]
    vmem = pl.BlockSpec(memory_space=pltpu.VMEM)
    return pl.pallas_call(
        project_body,
        in_specs=[pl.BlockSpec(memory_space=pltpu.SMEM)] * 2 + [vmem] * 7,
        out_shape=[jax.ShapeDtypeStruct(o, F32) for o in ((32, 128), (32, 128), (8, 128))],
        scratch_shapes=[
            pltpu.VMEM((count, HEADS * HD), BF),
            pltpu.VMEM((2, count, cols), F32),
            pltpu.VMEM((count, 128), F32),
        ],
        compiler_params=pltpu.CompilerParams(vmem_limit_bytes=12 * MIB),
        name="project",
    )(blk, head, att, wa, wb, scale, shift, fw, fb)


def finish_body(head_ref, own_ref, got_ref, const_ref, upper_ref, lower_ref):
    side = head_ref[0] % 2
    own, got = own_ref[...], got_ref[...]
    m_own, m_got = own[:, 64:65], got[:, 64:65]
    apart = m_own - m_got
    square = own[:, 96:97] + got[:, 96:97] + apart * apart * (D / 4)
    rstd = lax.rsqrt(square * (1.0 / D) + NORM_EPS)
    first, second = const_ref[0:1, :], const_ref[1:2, :]
    u_own = jnp.where(side == 0, first, second)
    u_got = jnp.where(side == 0, second, first)
    total = own + got + (0.5 * apart) * (u_own - u_got)
    out = (total * rstd + const_ref[2:3, :]).astype(BF)[:, :64]

    src = lax.broadcasted_iota(jnp.int32, (64, 128), 0)
    dst = lax.broadcasted_iota(jnp.int32, (64, 128), 1)
    place = (src % 2) * 32 + (src // 2 % 2) * 16 + src // 4
    to = lax.broadcasted_iota(jnp.int32, (16, 32), 0)
    row = lax.broadcasted_iota(jnp.int32, (16, 32), 1)
    acc = jnp.zeros((16, 128), F32)
    for j in range(2):
        perm = jnp.where(dst == place + 64 * j, 1.0, 0.0).astype(BF)
        pick = jnp.where(row == (to % 8 * 2 + to // 8) * 2 + j, 1.0, 0.0).astype(BF)
        lanes = jnp.dot(out, perm, preferred_element_type=F32).astype(BF)
        acc = acc + jnp.dot(pick, lanes, preferred_element_type=F32)
    upper_ref[...] = acc[:8].astype(BF)
    lower_ref[...] = acc[8:].astype(BF)


def finish(head, own, got, const):
    vmem = pl.BlockSpec(memory_space=pltpu.VMEM)
    return pl.pallas_call(
        finish_body,
        in_specs=[pl.BlockSpec(memory_space=pltpu.SMEM), vmem, vmem, vmem],
        out_shape=[jax.ShapeDtypeStruct((8, 128), BF)] * 2,
        compiler_params=pltpu.CompilerParams(vmem_limit_bytes=2 * MIB),
        name="finish",
    )(head, own, got, const)


def spread_body(*refs):
    o_ref = refs[-1]
    rows = jnp.concatenate([ref[...].astype(F32) for ref in refs[:-1]], axis=0).astype(BF)
    o_ref[...] = jnp.broadcast_to(rows[None], o_ref.shape)


def spread(*rows):
    return ones_call(spread_body, jax.ShapeDtypeStruct((N, 32, 128), BF), 2, "spread")(*rows)


def conv_body(blk_ref, head_ref, r_ref, k1_ref, b1_ref, k2_ref, b2_ref, o_ref, win, feat, w1, w2):
    blank = jnp.zeros((16, CH), BF)
    for a in range(3):
        for wr in range(4):
            for wc in range(4):
                ry, p = divmod(wr, 2)
                row = ((a * 2 + ry) * 4 + wc) * 32 + p * 16
                for ey in range(2):
                    for ex in range(2):
                        b, g = wr - ey, wc - ex
                        hit = 0 <= b < 3 and 0 <= g < 3
                        tile = k1_ref[(a * 3 + b) * 3 + g] if hit else blank
                        w1[pl.ds(row, 16), pl.ds((ey * 2 + ex) * CH, CH)] = tile
    taps = ((1, 0, None, 2), (2, 1, 0, None))
    blank = jnp.zeros((32, CH), BF)
    for a in range(3):
        for u, pair in enumerate(((2, None), (1, 2), (0, 1), (None, 0))):
            for ey, b in enumerate(pair):
                for qi in range(2):
                    for n, g in enumerate(taps[qi]):
                        hit = b is not None and g is not None
                        tile = k2_ref[(a * 3 + b) * 3 + g] if hit else blank
                        span = pl.ds((ey * 2 + qi) * CH, CH)
                        w2[a, pl.ds(u * 128 + n * 32, 32), span] = tile

    rows = r_ref[...].astype(F32).reshape(512, 128)
    lane = lax.broadcasted_iota(jnp.int32, (512, 128), 1)
    col = lax.broadcasted_iota(jnp.int32, (512, 128), 0) % 16
    before = jnp.where(col == 0, 0.0, pltpu.roll(rows, 1, 0))
    after = jnp.where(col == 15, 0.0, pltpu.roll(rows, 511, 0))
    views = (
        pltpu.roll(jnp.where(lane < 96, rows, before), 32, 1),
        pltpu.roll(jnp.where(lane < 32, after, rows), 96, 1),
    )
    for j, view in enumerate(views):
        view = view.astype(BF).reshape(4, 8, 16, 128)
        for r in range(3):
            for ry in range(2):
                span = pl.ds(ry * 128, 128)
                win[j, 2:, r, :, span] = view[r + ry]
                for early in range(2):
                    win[j, early, r, :, span] = view[r + ry, 0]

    top = jnp.where(blk_ref[0] == 0, 0.0, 1.0)
    bottom = jnp.where(blk_ref[0] == N - 1, 0.0, 1.0)
    for j in range(2):
        lhs = jnp.concatenate([win[j, a : a + 8] for a in range(3)], axis=-1)
        lhs = lhs.reshape(8 * 3 * 16, lhs.shape[-1])
        for n in range(4):
            span = pl.ds(n * CH, CH)
            v = jnp.dot(lhs, w1[:, span], preferred_element_type=F32) + b1_ref[...]
            v = (v / (1.0 + jnp.exp(-v))).reshape(8, 3, 16, CH)
            for r in range(3):
                f = v[:, r]
                if (r, n // 2) == (0, 0):
                    f = f * top
                if (r, n // 2) == (2, 1):
                    f = f * bottom
                f = f.astype(BF)
                feat[j, 2:, r, :, span] = f
                feat[j, 0, r, :, span] = f[0]
                feat[j, 1, r, :, span] = f[0]

    def product(a, r, first):
        lhs = feat[:, a : a + 8, r].reshape(256, 4 * CH)
        rhs = w2[a, pl.ds(first, 256), :]
        return lax.dot_general(lhs, rhs, (((1,), (1,)), ((), ())), preferred_element_type=F32)

    src = lax.broadcasted_iota(jnp.int32, (CH, 128), 0)
    dst = lax.broadcasted_iota(jnp.int32, (CH, 128), 1) % 32 + head_ref[0] * 32
    pick = jnp.where(src == dst, 1.0, 0.0).astype(BF)
    terms = jnp.concatenate(bf16_terms(b2_ref[...]) + [jnp.zeros((5, CH), F32)], axis=0)
    terms = jnp.dot(terms.astype(BF), pick, preferred_element_type=F32)
    bias = terms[0:1] + terms[1:2] + terms[2:3]

    lane = lax.broadcasted_iota(jnp.int32, (128, 128), 1)
    col = lax.broadcasted_iota(jnp.int32, (128, 128), 0) % 16
    for pair in range(2):
        acc = jnp.zeros((256, 256), F32)
        for a in range(3):
            acc = acc + product(a, pair, 256) + product(a, pair + 1, 0)
        for y in range(2):
            z = acc[:, y * 128 : (y + 1) * 128]
            z0, z1 = z[:128], z[128:]
            right = jnp.where(col == 0, 0.0, pltpu.roll(z1, 1, 0))
            left = jnp.where(col == 15, 0.0, pltpu.roll(z0, 127, 0))
            s0 = z0 + pltpu.roll(jnp.where(lane < 96, right, z1), 64, 1)
            s1 = z1 + pltpu.roll(jnp.where(lane < 96, z0, left), 64, 1)
            out = jnp.where(lane < 64, s0, pltpu.roll(s1, 64, 1)) + bias
            o_ref[pair * 2 + y] = out.astype(BF).reshape(8, 16, 128)


def conv_stage(blk, head, rows, k1, b1, k2, b2):
    vmem = pl.BlockSpec(memory_space=pltpu.VMEM)
    return pl.pallas_call(
        conv_body,
        in_specs=[pl.BlockSpec(memory_space=pltpu.SMEM)] * 2 + [vmem] * 5,
        out_shape=jax.ShapeDtypeStruct((4, 8, 16, 128), BF),
        scratch_shapes=[
            pltpu.VMEM((2, 10, 3, 16, 256), BF),
            pltpu.VMEM((2, 10, 3, 16, 4 * CH), BF),
            pltpu.VMEM((768, 4 * CH), BF),
            pltpu.VMEM((3, 512, 4 * CH), BF),
        ],
        compiler_params=pltpu.CompilerParams(vmem_limit_bytes=24 * MIB),
        name="convs",
    )(blk, head, rows, k1, b1, k2, b2)


def after(value, *others):
    return lax.optimization_barrier((value,) + others)[0]


def shards(
    qkv,
    query_blocks,
    out_weight,
    mod_shift,
    mod_scale,
    final_weight,
    final_bias,
    conv_in_weight,
    conv_in_bias,
    conv_weight,
    conv_bias,
):
    head = lax.axis_index("head")
    blk = lax.axis_index("blk")
    core = blk % 2
    side = head % 2
    blk_at, head_at = blk.reshape(1), head.reshape(1)

    q_send = split_heads(qkv, (0,))
    quarter = D // 4
    mine, theirs = (side * 2 + core) * quarter, ((1 - side) * 2 + core) * quarter
    source = after(out_weight, q_send)
    part = lax.dynamic_slice_in_dim(source, mine, quarter, axis=1)
    given = lax.dynamic_slice_in_dim(source, theirs, quarter, axis=1)
    pair = jnp.stack([part, lax.ppermute(given, "head", NEXT_SWAP)])

    q_all = lax.all_to_all(q_send, "head", 0, 0, tiled=True)
    kv_send = after(split_heads(qkv, (1, 2)), q_all, pair)
    kv_got = lax.all_to_all(kv_send, "head", 0, 0, tiled=True).reshape(-1, 2 * HD)
    weight_a = lax.all_gather(
        after(pair, kv_got), "head", axis=0, tiled=True, axis_index_groups=GROUPS_Z
    )

    near = select_queries(query_blocks, q_all)
    both = jnp.concatenate([near, lax.ppermute(near, "blk", FAR_SWAP)], axis=0)
    queries = [both]
    for m in range(1, 4):
        queries.append(lax.ppermute(both, "blk", Y_SWAPS[m]))
    kv_own = after(kv_got, *queries)
    kv_other = lax.ppermute(kv_own, "blk", NEXT_SWAP)

    keys, vals = pack(kv_own, kv_other)
    part_2 = attention(queries[2], keys, vals)
    got_2 = lax.ppermute(part_2, "blk", Y_SWAPS[2])
    part_1 = attention(after(queries[1], part_2), keys, vals)
    got_1 = lax.ppermute(part_1, "blk", Y_SWAPS[1])
    part_3 = attention(after(queries[3], part_1, got_2), keys, vals)
    got_3 = lax.ppermute(part_3, "blk", Y_SWAPS[3])
    part_0 = attention(after(queries[0], part_3, got_1), keys, vals)
    parts = (part_0, got_1, got_2, got_3)
    far_rows = lax.ppermute(merge(1, parts), "blk", FAR_SWAP)

    weight_a = after(weight_a, far_rows).reshape(HEADS * HD, quarter)
    weight_b = lax.ppermute(weight_a, "blk", NEXT_SWAP)

    attended = merge_last(merge(0, parts), far_rows)
    attended = lax.all_to_all(attended, "head", 0, 0, tiled=True)
    own, send, const = project(
        blk_at,
        head_at,
        attended,
        weight_a,
        weight_b,
        mod_scale.reshape(1, D),
        mod_shift.reshape(1, D),
        jnp.transpose(final_weight),
        final_bias.reshape(1, 64),
    )
    upper, lower = finish(head_at, own, lax.ppermute(send, "head", NEXT_SWAP), const)

    ends = N - 1
    above = lax.ppermute(lower, "blk", [(i, i + 1) for i in range(ends)])
    below = lax.ppermute(upper, "blk", [(i + 1, i) for i in range(ends)])
    rows = lax.all_to_all(spread(above, upper, lower, below), "head", 0, 0, tiled=True)
    out = conv_stage(
        blk_at,
        head_at,
        jnp.transpose(rows, (1, 0, 2)),
        conv_in_weight.reshape(27, 16, CH),
        conv_in_bias.reshape(1, CH),
        jnp.transpose(conv_weight, (0, 1, 2, 4, 3)).reshape(27, 32, CH),
        conv_bias.reshape(1, CH),
    )
    out = lax.all_to_all(jnp.transpose(out, (2, 0, 1, 3)), "head", 0, 0, tiled=True)
    out = jnp.transpose(out.reshape(N, 4, 8, 4, 32), (2, 1, 3, 0, 4))
    return out.reshape(8, 4, 4, CH)


def solution(mesh):
    in_specs = (
        P("blk", "head", None),
        P("blk"),
        P("head", None),
        P(),
        P(),
        P(),
        P(),
        P(),
        P(),
        P(None, None, None, None, "head"),
        P(),
    )
    out_specs = P(None, "blk", "head", None)
    return jax.shard_map(shards, mesh=mesh, in_specs=in_specs, out_specs=out_specs, check_vma=False)
```

```python
import functools
import math

import jax
import jax.numpy as jnp
from jax import lax
from jax.experimental import pallas as pl
from jax.experimental.pallas import tpu as pltpu
from jax.sharding import PartitionSpec as P

HEADS = 16
HD = 128
D = 3072
QBLK = 128
QROWS = 512
CH = 512
NORM_EPS = 1e-06
BF = jnp.bfloat16
F32 = jnp.float32
COEF = math.log2(math.e) / math.sqrt(HD)
MIB = 2**20

N = 16
GROUPS_Z = [[x + 2 * k for k in range(8)] for x in range(2)]
NEXT_SWAP = [(i, i ^ 1) for i in range(N)]
Y_SWAPS = [[(i, i ^ (2 * m)) for i in range(N)] for m in range(4)]
BOTH_SWAP = [(h * N + b, (h ^ 1) * N + (b ^ 1)) for h in range(N) for b in range(N)]
FAR_SWAP = [(i, i ^ 8) for i in range(N)]


def ones_call(body, out_shape, limit, name):
    return pl.pallas_call(
        body,
        out_shape=out_shape,
        compiler_params=pltpu.CompilerParams(vmem_limit_bytes=limit * MIB),
        name=name,
    )


def split_body(*refs):
    o_ref = refs[-1]
    for n, ref in enumerate(refs[:-1]):
        for h in range(HEADS):
            o_ref[h, :, n * HD : (n + 1) * HD] = ref[0, :, h * HD : (h + 1) * HD]


def split_heads(qkv, parts):
    tok = qkv.shape[1]
    return pl.pallas_call(
        split_body,
        grid=(1,),
        in_specs=[
            pl.BlockSpec((1, tok, HEADS * HD), lambda i, p=p: (0, 0, p)) for p in parts
        ],
        out_specs=pl.BlockSpec((HEADS, tok, len(parts) * HD), lambda i: (0, 0, 0)),
        out_shape=jax.ShapeDtypeStruct((HEADS, tok, len(parts) * HD), BF),
        compiler_params=pltpu.CompilerParams(vmem_limit_bytes=56 * MIB),
        name="split",
    )(*[qkv] * len(parts))


def select_body(chosen_ref, q_ref, o_ref):
    for i in range(QROWS // QBLK):
        o_ref[pl.ds(i * QBLK, QBLK), :] = q_ref[chosen_ref[i] % N]


def select_queries(chosen, q_all):
    return pl.pallas_call(
        select_body,
        in_specs=[
            pl.BlockSpec(memory_space=pltpu.SMEM),
            pl.BlockSpec(memory_space=pltpu.VMEM),
        ],
        out_shape=jax.ShapeDtypeStruct((QROWS, HD), BF),
        compiler_params=pltpu.CompilerParams(vmem_limit_bytes=4 * MIB),
        name="select",
    )(chosen, q_all)


def pack_body(own_ref, other_ref, keys, vals):
    half = own_ref.shape[0]
    for s, ref in enumerate((own_ref, other_ref)):
        rows = pl.ds(s * half, half)
        keys[rows, :HD] = ref[:, :HD]
        keys[rows, HD:] = ref[:, :HD]
        vals[rows, :HD] = ref[:, HD:]
        vals[rows, HD:] = jnp.ones((half, HD), BF)


def pack(own, other):
    shape = jax.ShapeDtypeStruct((2 * own.shape[0], 2 * HD), BF)
    return ones_call(pack_body, [shape, shape], 8, "pack")(own, other)


def store_lse(o_ref, chunk, lse):
    hi = lse.astype(BF).astype(F32)
    mid = (lse - hi).astype(BF).astype(F32)
    low = lse - hi - mid
    tail = jnp.concatenate([hi, mid, low, jnp.zeros_like(hi)], axis=0)
    o_ref[chunk, QROWS:, :] = tail.astype(BF)


def load_lse(ref, s):
    tail = ref[s, QROWS:, :].astype(F32)
    return tail[0:4] + tail[4:8] + tail[8:12]


def column(row):
    return jnp.transpose(jnp.broadcast_to(row, (128, 128)))


def attention_body(sub, q_ref, keys, vals, o_ref):
    def scores(chunk, first):
        q = q_ref[pl.ds(chunk * QROWS + first, sub), :].astype(F32) * COEF
        hi = q.astype(BF)
        lo = (q - hi.astype(F32)).astype(BF)
        return lax.dot_general(
            jnp.concatenate([hi, lo], axis=1),
            keys[...],
            (((1,), (1,)), ((), ())),
            preferred_element_type=F32,
        )

    tiles = [(chunk, first) for chunk in range(2) for first in range(0, QROWS, sub)]
    lse_rows = []
    current = scores(*tiles[0])
    for n, (chunk, first) in enumerate(tiles):
        later = scores(*tiles[n + 1]) if n + 1 < len(tiles) else None
        high = jnp.max(current, axis=1, keepdims=True)
        weights = jnp.exp2(current - high).astype(BF)
        acc = jnp.dot(weights, vals[...], preferred_element_type=F32)
        total = acc[:, HD:]
        o_ref[chunk, first : first + sub, :] = (acc[:, :HD] / total).astype(BF)
        lse = high + jnp.log2(total)
        for k in range(sub // 128):
            lse_rows.append(jnp.transpose(lse[k * 128 : (k + 1) * 128])[:1])
        if first + sub == QROWS:
            store_lse(o_ref, chunk, jnp.concatenate(lse_rows, axis=0))
            lse_rows = []
        current = later


def attention(queries, keys, vals):
    count = keys.shape[0]
    return pl.pallas_call(
        functools.partial(attention_body, 256),
        in_specs=[pl.BlockSpec(memory_space=pltpu.VMEM)] * 3,
        out_shape=jax.ShapeDtypeStruct((2, QROWS + 16, HD), BF),
        compiler_params=pltpu.CompilerParams(vmem_limit_bytes=24 * MIB),
        cost_estimate=pl.CostEstimate(
            flops=12 * 2 * QROWS * count * 2 * HD,
            bytes_accessed=4 * MIB,
            transcendentals=2 * QROWS * count,
        ),
        name="attention",
    )(queries, keys, vals)


def merged(refs, n):
    lses = [load_lse(ref, n) for ref in refs]
    high = functools.reduce(jnp.maximum, lses)
    shares = [jnp.exp2(v - high) for v in lses]
    total = functools.reduce(jnp.add, shares)
    shares = [v / total for v in shares]
    blocks = []
    for k in range(4):
        acc = jnp.zeros((128, HD), F32)
        for share, ref in zip(shares, refs):
            part = ref[n, pl.ds(k * 128, 128), :].astype(F32)
            acc = acc + column(share[k : k + 1]) * part
        blocks.append(acc.astype(BF))
    return blocks, high + jnp.log2(total)


def merge_body(n, *refs):
    o_ref = refs[-1]
    blocks, lse = merged(refs[:-1], n)
    for k, block in enumerate(blocks):
        o_ref[0, pl.ds(k * 128, 128), :] = block
    store_lse(o_ref, 0, lse)


def merge(n, parts):
    shape = jax.ShapeDtypeStruct((1, QROWS + 16, HD), BF)
    return ones_call(functools.partial(merge_body, n), shape, 8, "merge")(*parts)


def merge_last_body(a_ref, b_ref, o_ref):
    blocks, _ = merged((a_ref, b_ref), 0)
    for k, block in enumerate(blocks):
        for n in range(4):
            o_ref[k * 4 + n] = block[n // 2 * 64 : n // 2 * 64 + 64]


def merge_last(a, b):
    shape = jax.ShapeDtypeStruct((N, 64, HD), BF)
    return ones_call(merge_last_body, shape, 8, "merge_last")(a, b)


def bf16_terms(v):
    hi = v.astype(BF).astype(F32)
    mid = (v - hi).astype(BF).astype(F32)
    return [hi, mid, v - hi - mid]


def project_body(
    blk_ref, head_ref, att_ref, other_ref, w_ref, scale_ref, shift_ref, fw_ref, fb_ref, *refs
):
    own_ref, side_ref, core_ref, both_ref, const_ref, rows, stats = refs
    core, side = blk_ref[0] % 2, head_ref[0] % 2
    count, cols = att_ref.shape[1], w_ref.shape[1]
    contract = (((1,), (1,)), ((), ()))
    for h in range(HEADS):
        rows[:count, h * HD : (h + 1) * HD] = att_ref[h ^ side]
        rows[count:, h * HD : (h + 1) * HD] = other_ref[h ^ side]
    x = jnp.dot(rows[...], w_ref[...], preferred_element_type=F32)

    moved = jnp.zeros((1, 128), F32)
    blank = jnp.zeros((64, cols), BF)
    for s in range(4):
        span = pl.ds(s * cols, cols)
        terms = bf16_terms(1.0 + scale_ref[:, span]) + bf16_terms(shift_ref[:, span])
        lhs = jnp.concatenate(terms + [jnp.zeros((2, cols), F32)], axis=0).astype(BF)
        rhs = jnp.concatenate([fw_ref[:, span], blank], axis=0)
        got = lax.dot_general(lhs, rhs, contract, preferred_element_type=F32)
        const_ref[s : s + 1, :] = got[0:1] + got[1:2] + got[2:3]
        moved = moved + got[3:4] + got[4:5] + got[5:6]
    const_ref[4:5, :] = moved
    const_ref[4:5, :64] = moved[:, :64] + fb_ref[...]

    mean = jnp.sum(x, axis=1, keepdims=True) * (1.0 / cols)
    x = x - mean
    square = jnp.sum(x * x, axis=1, keepdims=True)
    span = pl.ds(pl.multiple_of((side * 2 + core) * cols, 128), cols)
    m = (x * (1.0 + scale_ref[:, span])).astype(BF)
    rhs = jnp.concatenate([fw_ref[:, span], blank], axis=0)
    acc = lax.dot_general(m, rhs, contract, preferred_element_type=F32)
    lane = lax.broadcasted_iota(jnp.int32, stats.shape, 1)
    stats[...] = jnp.where(lane < 64, acc, jnp.where(lane < 96, mean, square))
    mine, theirs = pl.multiple_of(side * 32, 32), pl.multiple_of(32 - side * 32, 32)
    own_ref[...] = stats[pl.ds(mine, 32), :]
    side_ref[...] = stats[pl.ds(theirs, 32), :]
    core_ref[...] = stats[pl.ds(count + mine, 32), :]
    both_ref[...] = stats[pl.ds(count + theirs, 32), :]


def project(blk, head, att, other, w, scale, shift, fw, fb):
    count = att.shape[1]
    vmem = pl.BlockSpec(memory_space=pltpu.VMEM)
    outs = [(32, 128)] * 4 + [(8, 128)]
    return pl.pallas_call(
        project_body,
        in_specs=[pl.BlockSpec(memory_space=pltpu.SMEM)] * 2 + [vmem] * 7,
        out_shape=[jax.ShapeDtypeStruct(o, F32) for o in outs],
        scratch_shapes=[
            pltpu.VMEM((2 * count, HEADS * HD), BF),
            pltpu.VMEM((2 * count, 128), F32),
        ],
        compiler_params=pltpu.CompilerParams(vmem_limit_bytes=12 * MIB),
        name="project",
    )(blk, head, att, other, w, scale, shift, fw, fb)


def finish_body(blk_ref, head_ref, *refs):
    const_ref, upper_ref, lower_ref = refs[4:]
    core, side = blk_ref[0] % 2, head_ref[0] % 2
    parts = [ref[...] for ref in refs[:4]]
    places = [(side, core), (1 - side, core), (side, 1 - core), (1 - side, 1 - core)]
    means = [part[:, 64:65] for part in parts]
    mean = sum(means) * 0.25
    total = sum(parts)
    square = total[:, 96:97]
    for (s, c), own in zip(places, means):
        apart = own - mean
        square = square + apart * apart * (D / 4)
        total = total + apart * const_ref[pl.ds(s * 2 + c, 1), :]
    rstd = lax.rsqrt(square * (1.0 / D) + NORM_EPS)
    out = (total * rstd + const_ref[4:5, :]).astype(BF)[:, :64]

    src = lax.broadcasted_iota(jnp.int32, (64, 128), 0)
    dst = lax.broadcasted_iota(jnp.int32, (64, 128), 1)
    place = (src % 2) * 32 + (src // 2 % 2) * 16 + src // 4
    to = lax.broadcasted_iota(jnp.int32, (16, 32), 0)
    row = lax.broadcasted_iota(jnp.int32, (16, 32), 1)
    acc = jnp.zeros((16, 128), F32)
    for j in range(2):
        perm = jnp.where(dst == place + 64 * j, 1.0, 0.0).astype(BF)
        pick = jnp.where(row == (to % 8 * 2 + to // 8) * 2 + j, 1.0, 0.0).astype(BF)
        lanes = jnp.dot(out, perm, preferred_element_type=F32).astype(BF)
        acc = acc + jnp.dot(pick, lanes, preferred_element_type=F32)
    upper_ref[...] = acc[:8].astype(BF)
    lower_ref[...] = acc[8:].astype(BF)


def finish(blk, head, parts, const):
    vmem = pl.BlockSpec(memory_space=pltpu.VMEM)
    return pl.pallas_call(
        finish_body,
        in_specs=[pl.BlockSpec(memory_space=pltpu.SMEM)] * 2 + [vmem] * 5,
        out_shape=[jax.ShapeDtypeStruct((8, 128), BF)] * 2,
        compiler_params=pltpu.CompilerParams(vmem_limit_bytes=2 * MIB),
        name="finish",
    )(blk, head, *parts, const)


def spread_body(*refs):
    o_ref = refs[-1]
    rows = jnp.concatenate([ref[...].astype(F32) for ref in refs[:-1]], axis=0).astype(BF)
    o_ref[...] = jnp.broadcast_to(rows[None], o_ref.shape)


def spread(*rows):
    return ones_call(spread_body, jax.ShapeDtypeStruct((N, 32, 128), BF), 2, "spread")(*rows)


def conv_body(blk_ref, head_ref, r_ref, k1_ref, b1_ref, k2_ref, b2_ref, o_ref, win, feat, w1, w2):
    blank = jnp.zeros((16, CH), BF)
    for a in range(3):
        for wr in range(4):
            for wc in range(4):
                ry, p = divmod(wr, 2)
                row = ((a * 2 + ry) * 4 + wc) * 32 + p * 16
                for ey in range(2):
                    for ex in range(2):
                        b, g = wr - ey, wc - ex
                        hit = 0 <= b < 3 and 0 <= g < 3
                        tile = k1_ref[(a * 3 + b) * 3 + g] if hit else blank
                        w1[pl.ds(row, 16), pl.ds((ey * 2 + ex) * CH, CH)] = tile
    taps = ((1, 0, None, 2), (2, 1, 0, None))
    blank = jnp.zeros((32, CH), BF)
    for a in range(3):
        for u, pair in enumerate(((2, None), (1, 2), (0, 1), (None, 0))):
            for ey, b in enumerate(pair):
                for qi in range(2):
                    for n, g in enumerate(taps[qi]):
                        hit = b is not None and g is not None
                        tile = k2_ref[(a * 3 + b) * 3 + g] if hit else blank
                        span = pl.ds((ey * 2 + qi) * CH, CH)
                        w2[a, pl.ds(u * 128 + n * 32, 32), span] = tile

    rows = r_ref[...].astype(F32).reshape(512, 128)
    lane = lax.broadcasted_iota(jnp.int32, (512, 128), 1)
    col = lax.broadcasted_iota(jnp.int32, (512, 128), 0) % 16
    before = jnp.where(col == 0, 0.0, pltpu.roll(rows, 1, 0))
    after = jnp.where(col == 15, 0.0, pltpu.roll(rows, 511, 0))
    views = (
        pltpu.roll(jnp.where(lane < 96, rows, before), 32, 1),
        pltpu.roll(jnp.where(lane < 32, after, rows), 96, 1),
    )
    for j, view in enumerate(views):
        view = view.astype(BF).reshape(4, 8, 16, 128)
        for r in range(3):
            for ry in range(2):
                span = pl.ds(ry * 128, 128)
                win[j, 2:, r, :, span] = view[r + ry]
                for early in range(2):
                    win[j, early, r, :, span] = view[r + ry, 0]

    top = jnp.where(blk_ref[0] == 0, 0.0, 1.0)
    bottom = jnp.where(blk_ref[0] == N - 1, 0.0, 1.0)
    for j in range(2):
        lhs = jnp.concatenate([win[j, a : a + 8] for a in range(3)], axis=-1)
        lhs = lhs.reshape(8 * 3 * 16, lhs.shape[-1])
        for n in range(4):
            span = pl.ds(n * CH, CH)
            v = jnp.dot(lhs, w1[:, span], preferred_element_type=F32) + b1_ref[...]
            v = (v / (1.0 + jnp.exp(-v))).reshape(8, 3, 16, CH)
            for r in range(3):
                f = v[:, r]
                if (r, n // 2) == (0, 0):
                    f = f * top
                if (r, n // 2) == (2, 1):
                    f = f * bottom
                f = f.astype(BF)
                feat[j, 2:, r, :, span] = f
                feat[j, 0, r, :, span] = f[0]
                feat[j, 1, r, :, span] = f[0]

    def product(a, r, first):
        lhs = feat[:, a : a + 8, r].reshape(256, 4 * CH)
        rhs = w2[a, pl.ds(first, 256), :]
        return lax.dot_general(lhs, rhs, (((1,), (1,)), ((), ())), preferred_element_type=F32)

    src = lax.broadcasted_iota(jnp.int32, (CH, 128), 0)
    dst = lax.broadcasted_iota(jnp.int32, (CH, 128), 1) % 32 + head_ref[0] * 32
    pick = jnp.where(src == dst, 1.0, 0.0).astype(BF)
    terms = jnp.concatenate(bf16_terms(b2_ref[...]) + [jnp.zeros((5, CH), F32)], axis=0)
    terms = jnp.dot(terms.astype(BF), pick, preferred_element_type=F32)
    bias = terms[0:1] + terms[1:2] + terms[2:3]

    lane = lax.broadcasted_iota(jnp.int32, (128, 128), 1)
    col = lax.broadcasted_iota(jnp.int32, (128, 128), 0) % 16
    for pair in range(2):
        acc = jnp.zeros((256, 256), F32)
        for a in range(3):
            acc = acc + product(a, pair, 256) + product(a, pair + 1, 0)
        for y in range(2):
            z = acc[:, y * 128 : (y + 1) * 128]
            z0, z1 = z[:128], z[128:]
            right = jnp.where(col == 0, 0.0, pltpu.roll(z1, 1, 0))
            left = jnp.where(col == 15, 0.0, pltpu.roll(z0, 127, 0))
            s0 = z0 + pltpu.roll(jnp.where(lane < 96, right, z1), 64, 1)
            s1 = z1 + pltpu.roll(jnp.where(lane < 96, z0, left), 64, 1)
            out = jnp.where(lane < 64, s0, pltpu.roll(s1, 64, 1)) + bias
            o_ref[pair * 2 + y] = out.astype(BF).reshape(8, 16, 128)


def conv_stage(blk, head, rows, k1, b1, k2, b2):
    vmem = pl.BlockSpec(memory_space=pltpu.VMEM)
    return pl.pallas_call(
        conv_body,
        in_specs=[pl.BlockSpec(memory_space=pltpu.SMEM)] * 2 + [vmem] * 5,
        out_shape=jax.ShapeDtypeStruct((4, 8, 16, 128), BF),
        scratch_shapes=[
            pltpu.VMEM((2, 10, 3, 16, 256), BF),
            pltpu.VMEM((2, 10, 3, 16, 4 * CH), BF),
            pltpu.VMEM((768, 4 * CH), BF),
            pltpu.VMEM((3, 512, 4 * CH), BF),
        ],
        compiler_params=pltpu.CompilerParams(vmem_limit_bytes=24 * MIB),
        name="convs",
    )(blk, head, rows, k1, b1, k2, b2)


def after(value, *others):
    return lax.optimization_barrier((value,) + others)[0]


def shards(
    qkv,
    query_blocks,
    out_weight,
    mod_shift,
    mod_scale,
    final_weight,
    final_bias,
    conv_in_weight,
    conv_in_bias,
    conv_weight,
    conv_bias,
):
    head = lax.axis_index("head")
    blk = lax.axis_index("blk")
    core = blk % 2
    side = head % 2
    blk_at, head_at = blk.reshape(1), head.reshape(1)

    q_send = split_heads(qkv, (0,))
    quarter = D // 4
    mine, theirs = (side * 2 + core) * quarter, ((1 - side) * 2 + core) * quarter
    source = after(out_weight, q_send)
    part = lax.dynamic_slice_in_dim(source, mine, quarter, axis=1)
    given = lax.dynamic_slice_in_dim(source, theirs, quarter, axis=1)
    pair = jnp.stack([part, lax.ppermute(given, "head", NEXT_SWAP)])

    q_all = lax.all_to_all(q_send, "head", 0, 0, tiled=True)
    kv_send = after(split_heads(qkv, (1, 2)), q_all, pair)
    kv_got = lax.all_to_all(kv_send, "head", 0, 0, tiled=True).reshape(-1, 2 * HD)
    weight_a = lax.all_gather(
        after(pair, kv_got), "head", axis=0, tiled=True, axis_index_groups=GROUPS_Z
    )

    near = select_queries(query_blocks, q_all)
    both = jnp.concatenate([near, lax.ppermute(near, "blk", FAR_SWAP)], axis=0)
    queries = [both]
    for m in range(1, 4):
        queries.append(lax.ppermute(both, "blk", Y_SWAPS[m]))
    kv_own = after(kv_got, *queries)
    kv_other = lax.ppermute(kv_own, "blk", NEXT_SWAP)

    keys, vals = pack(kv_own, kv_other)
    part_2 = attention(queries[2], keys, vals)
    got_2 = lax.ppermute(part_2, "blk", Y_SWAPS[2])
    part_1 = attention(after(queries[1], part_2), keys, vals)
    got_1 = lax.ppermute(part_1, "blk", Y_SWAPS[1])
    part_3 = attention(after(queries[3], part_1, got_2), keys, vals)
    got_3 = lax.ppermute(part_3, "blk", Y_SWAPS[3])
    part_0 = attention(after(queries[0], part_3, got_1), keys, vals)
    parts = (part_0, got_1, got_2, got_3)
    far_rows = lax.ppermute(merge(1, parts), "blk", FAR_SWAP)

    attended = merge_last(merge(0, parts), far_rows)
    attended = lax.all_to_all(attended, "head", 0, 0, tiled=True)
    other = lax.ppermute(attended, "blk", NEXT_SWAP)
    weight = after(weight_a, attended).reshape(HEADS * HD, quarter)
    own, to_side, to_core, to_both, const = project(
        blk_at,
        head_at,
        attended,
        other,
        weight,
        mod_scale.reshape(1, D),
        mod_shift.reshape(1, D),
        jnp.transpose(final_weight),
        final_bias.reshape(1, 64),
    )
    shares = (
        own,
        lax.ppermute(to_side, "head", NEXT_SWAP),
        lax.ppermute(to_core, "blk", NEXT_SWAP),
        lax.ppermute(to_both, ("head", "blk"), BOTH_SWAP),
    )
    upper, lower = finish(blk_at, head_at, shares, const)

    ends = N - 1
    above = lax.ppermute(lower, "blk", [(i, i + 1) for i in range(ends)])
    below = lax.ppermute(upper, "blk", [(i + 1, i) for i in range(ends)])
    rows = lax.all_to_all(spread(above, upper, lower, below), "head", 0, 0, tiled=True)
    out = conv_stage(
        blk_at,
        head_at,
        jnp.transpose(rows, (1, 0, 2)),
        conv_in_weight.reshape(27, 16, CH),
        conv_in_bias.reshape(1, CH),
        jnp.transpose(conv_weight, (0, 1, 2, 4, 3)).reshape(27, 32, CH),
        conv_bias.reshape(1, CH),
    )
    out = lax.all_to_all(jnp.transpose(out, (2, 0, 1, 3)), "head", 0, 0, tiled=True)
    out = jnp.transpose(out.reshape(N, 4, 8, 4, 32), (2, 1, 3, 0, 4))
    return out.reshape(8, 4, 4, CH)


def solution(mesh):
    in_specs = (
        P("blk", "head", None),
        P("blk"),
        P("head", None),
        P(),
        P(),
        P(),
        P(),
        P(),
        P(),
        P(None, None, None, None, "head"),
        P(),
    )
    out_specs = P(None, "blk", "head", None)
    return jax.shard_map(shards, mesh=mesh, in_specs=in_specs, out_specs=out_specs, check_vma=False)
```

```python
import functools
import math

import jax
import jax.numpy as jnp
from jax import lax
from jax.experimental import pallas as pl
from jax.experimental.pallas import tpu as pltpu
from jax.sharding import PartitionSpec as P

HEADS = 16
HD = 128
D = 3072
QBLK = 128
QROWS = 512
CH = 512
NORM_EPS = 1e-06
BF = jnp.bfloat16
F32 = jnp.float32
COEF = math.log2(math.e) / math.sqrt(HD)
MIB = 2**20

N = 16
GROUPS_Z = [[x + 2 * k for k in range(8)] for x in range(2)]
NEXT_SWAP = [(i, i ^ 1) for i in range(N)]
Y_SWAPS = [[(i, i ^ (2 * m)) for i in range(N)] for m in range(4)]
BOTH_SWAP = [(h * N + b, (h ^ 1) * N + (b ^ 1)) for h in range(N) for b in range(N)]
FAR_SWAP = [(i, i ^ 8) for i in range(N)]


def ones_call(body, out_shape, limit, name):
    return pl.pallas_call(
        body,
        out_shape=out_shape,
        compiler_params=pltpu.CompilerParams(vmem_limit_bytes=limit * MIB),
        name=name,
    )


def split_body(*refs):
    o_ref = refs[-1]
    for n, ref in enumerate(refs[:-1]):
        for h in range(HEADS):
            o_ref[h, :, n * HD : (n + 1) * HD] = ref[0, :, h * HD : (h + 1) * HD]


def split_heads(qkv, parts):
    tok = qkv.shape[1]
    return pl.pallas_call(
        split_body,
        grid=(1,),
        in_specs=[
            pl.BlockSpec((1, tok, HEADS * HD), lambda i, p=p: (0, 0, p)) for p in parts
        ],
        out_specs=pl.BlockSpec((HEADS, tok, len(parts) * HD), lambda i: (0, 0, 0)),
        out_shape=jax.ShapeDtypeStruct((HEADS, tok, len(parts) * HD), BF),
        compiler_params=pltpu.CompilerParams(vmem_limit_bytes=56 * MIB),
        name="split",
    )(*[qkv] * len(parts))


def select_body(chosen_ref, q_ref, o_ref):
    for i in range(QROWS // QBLK):
        o_ref[pl.ds(i * QBLK, QBLK), :] = q_ref[chosen_ref[i] % N]


def select_queries(chosen, q_all):
    return pl.pallas_call(
        select_body,
        in_specs=[
            pl.BlockSpec(memory_space=pltpu.SMEM),
            pl.BlockSpec(memory_space=pltpu.VMEM),
        ],
        out_shape=jax.ShapeDtypeStruct((QROWS, HD), BF),
        compiler_params=pltpu.CompilerParams(vmem_limit_bytes=4 * MIB),
        name="select",
    )(chosen, q_all)


def pack_body(own_ref, other_ref, keys, vals):
    half = own_ref.shape[0]
    for s, ref in enumerate((own_ref, other_ref)):
        rows = pl.ds(s * half, half)
        keys[rows, :HD] = ref[:, :HD]
        keys[rows, HD:] = ref[:, :HD]
        vals[rows, :HD] = ref[:, HD:]
        vals[rows, HD:] = jnp.ones((half, HD), BF)


def pack(own, other):
    shape = jax.ShapeDtypeStruct((2 * own.shape[0], 2 * HD), BF)
    return ones_call(pack_body, [shape, shape], 8, "pack")(own, other)


def store_lse(o_ref, chunk, lse):
    hi = lse.astype(BF).astype(F32)
    mid = (lse - hi).astype(BF).astype(F32)
    low = lse - hi - mid
    tail = jnp.concatenate([hi, mid, low, jnp.zeros_like(hi)], axis=0)
    o_ref[chunk, QROWS:, :] = tail.astype(BF)


def load_lse(ref, s):
    tail = ref[s, QROWS:, :].astype(F32)
    return tail[0:4] + tail[4:8] + tail[8:12]


def column(row):
    return jnp.transpose(jnp.broadcast_to(row, (128, 128)))


def attention_body(sub, q_ref, keys, vals, o_ref):
    def scores(chunk, first):
        q = q_ref[pl.ds(chunk * QROWS + first, sub), :].astype(F32) * COEF
        hi = q.astype(BF)
        lo = (q - hi.astype(F32)).astype(BF)
        return lax.dot_general(
            jnp.concatenate([hi, lo], axis=1),
            keys[...],
            (((1,), (1,)), ((), ())),
            preferred_element_type=F32,
        )

    tiles = [(chunk, first) for chunk in range(2) for first in range(0, QROWS, sub)]
    lse_rows = []
    current = scores(*tiles[0])
    for n, (chunk, first) in enumerate(tiles):
        later = scores(*tiles[n + 1]) if n + 1 < len(tiles) else None
        high = jnp.max(current, axis=1, keepdims=True)
        weights = jnp.exp2(current - high).astype(BF)
        acc = jnp.dot(weights, vals[...], preferred_element_type=F32)
        total = acc[:, HD:]
        o_ref[chunk, first : first + sub, :] = (acc[:, :HD] / total).astype(BF)
        lse = high + jnp.log2(total)
        for k in range(sub // 128):
            lse_rows.append(jnp.transpose(lse[k * 128 : (k + 1) * 128])[:1])
        if first + sub == QROWS:
            store_lse(o_ref, chunk, jnp.concatenate(lse_rows, axis=0))
            lse_rows = []
        current = later


def attention(queries, keys, vals):
    count = keys.shape[0]
    return pl.pallas_call(
        functools.partial(attention_body, 256),
        in_specs=[pl.BlockSpec(memory_space=pltpu.VMEM)] * 3,
        out_shape=jax.ShapeDtypeStruct((2, QROWS + 16, HD), BF),
        compiler_params=pltpu.CompilerParams(vmem_limit_bytes=24 * MIB),
        cost_estimate=pl.CostEstimate(
            flops=12 * 2 * QROWS * count * 2 * HD,
            bytes_accessed=4 * MIB,
            transcendentals=2 * QROWS * count,
        ),
        name="attention",
    )(queries, keys, vals)


def merged(refs, n):
    lses = [load_lse(ref, n) for ref in refs]
    high = functools.reduce(jnp.maximum, lses)
    shares = [jnp.exp2(v - high) for v in lses]
    total = functools.reduce(jnp.add, shares)
    shares = [v / total for v in shares]
    blocks = []
    for k in range(4):
        acc = jnp.zeros((128, HD), F32)
        for share, ref in zip(shares, refs):
            part = ref[n, pl.ds(k * 128, 128), :].astype(F32)
            acc = acc + column(share[k : k + 1]) * part
        blocks.append(acc.astype(BF))
    return blocks, high + jnp.log2(total)


def merge_body(n, *refs):
    o_ref = refs[-1]
    blocks, lse = merged(refs[:-1], n)
    for k, block in enumerate(blocks):
        o_ref[0, pl.ds(k * 128, 128), :] = block
    store_lse(o_ref, 0, lse)


def merge(n, parts):
    shape = jax.ShapeDtypeStruct((1, QROWS + 16, HD), BF)
    return ones_call(functools.partial(merge_body, n), shape, 8, "merge")(*parts)


def merge_last_body(a_ref, b_ref, o_ref):
    blocks, _ = merged((a_ref, b_ref), 0)
    for k, block in enumerate(blocks):
        for n in range(4):
            o_ref[k * 4 + n] = block[n // 2 * 64 : n // 2 * 64 + 64]


def merge_last(a, b):
    shape = jax.ShapeDtypeStruct((N, 64, HD), BF)
    return ones_call(merge_last_body, shape, 8, "merge_last")(a, b)


def bf16_terms(v):
    hi = v.astype(BF).astype(F32)
    mid = (v - hi).astype(BF).astype(F32)
    return [hi, mid, v - hi - mid]


def project_body(
    blk_ref, head_ref, att_ref, other_ref, w_ref, scale_ref, shift_ref, fw_ref, fb_ref, *refs
):
    own_ref, side_ref, core_ref, both_ref, const_ref, rows, stats = refs
    core, side = blk_ref[0] % 2, head_ref[0] % 2
    count, cols = att_ref.shape[1], w_ref.shape[1]
    contract = (((1,), (1,)), ((), ()))
    for h in range(HEADS):
        rows[:count, h * HD : (h + 1) * HD] = att_ref[h ^ side]
        rows[count:, h * HD : (h + 1) * HD] = other_ref[h ^ side]
    x = jnp.dot(rows[...], w_ref[...], preferred_element_type=F32)

    moved = jnp.zeros((1, 128), F32)
    blank = jnp.zeros((64, cols), BF)
    for s in range(4):
        span = pl.ds(s * cols, cols)
        terms = bf16_terms(1.0 + scale_ref[:, span]) + bf16_terms(shift_ref[:, span])
        lhs = jnp.concatenate(terms + [jnp.zeros((2, cols), F32)], axis=0).astype(BF)
        rhs = jnp.concatenate([fw_ref[:, span], blank], axis=0)
        got = lax.dot_general(lhs, rhs, contract, preferred_element_type=F32)
        const_ref[s : s + 1, :] = got[0:1] + got[1:2] + got[2:3]
        moved = moved + got[3:4] + got[4:5] + got[5:6]
    const_ref[4:5, :] = moved
    const_ref[4:5, :64] = moved[:, :64] + fb_ref[...]

    mean = jnp.sum(x, axis=1, keepdims=True) * (1.0 / cols)
    x = x - mean
    square = jnp.sum(x * x, axis=1, keepdims=True)
    span = pl.ds(pl.multiple_of((side * 2 + core) * cols, 128), cols)
    m = (x * (1.0 + scale_ref[:, span])).astype(BF)
    rhs = jnp.concatenate([fw_ref[:, span], blank], axis=0)
    acc = lax.dot_general(m, rhs, contract, preferred_element_type=F32)
    lane = lax.broadcasted_iota(jnp.int32, stats.shape, 1)
    stats[...] = jnp.where(lane < 64, acc, jnp.where(lane < 96, mean, square))
    mine, theirs = pl.multiple_of(side * 32, 32), pl.multiple_of(32 - side * 32, 32)
    own_ref[...] = stats[pl.ds(mine, 32), :]
    side_ref[...] = stats[pl.ds(theirs, 32), :]
    core_ref[...] = stats[pl.ds(count + mine, 32), :]
    both_ref[...] = stats[pl.ds(count + theirs, 32), :]


def project(blk, head, att, other, w, scale, shift, fw, fb):
    count = att.shape[1]
    vmem = pl.BlockSpec(memory_space=pltpu.VMEM)
    outs = [(32, 128)] * 4 + [(8, 128)]
    return pl.pallas_call(
        project_body,
        in_specs=[pl.BlockSpec(memory_space=pltpu.SMEM)] * 2 + [vmem] * 7,
        out_shape=[jax.ShapeDtypeStruct(o, F32) for o in outs],
        scratch_shapes=[
            pltpu.VMEM((2 * count, HEADS * HD), BF),
            pltpu.VMEM((2 * count, 128), F32),
        ],
        compiler_params=pltpu.CompilerParams(vmem_limit_bytes=12 * MIB),
        name="project",
    )(blk, head, att, other, w, scale, shift, fw, fb)


def finish_body(blk_ref, head_ref, *refs):
    const_ref, upper_ref, lower_ref = refs[4:]
    core, side = blk_ref[0] % 2, head_ref[0] % 2
    parts = [ref[...] for ref in refs[:4]]
    places = [(side, core), (1 - side, core), (side, 1 - core), (1 - side, 1 - core)]
    means = [part[:, 64:65] for part in parts]
    mean = sum(means) * 0.25
    total = sum(parts)
    square = total[:, 96:97]
    for (s, c), own in zip(places, means):
        apart = own - mean
        square = square + apart * apart * (D / 4)
        total = total + apart * const_ref[pl.ds(s * 2 + c, 1), :]
    rstd = lax.rsqrt(square * (1.0 / D) + NORM_EPS)
    out = (total * rstd + const_ref[4:5, :]).astype(BF)[:, :64]

    src = lax.broadcasted_iota(jnp.int32, (64, 128), 0)
    dst = lax.broadcasted_iota(jnp.int32, (64, 128), 1)
    place = (src % 2) * 32 + (src // 2 % 2) * 16 + src // 4
    to = lax.broadcasted_iota(jnp.int32, (16, 32), 0)
    row = lax.broadcasted_iota(jnp.int32, (16, 32), 1)
    acc = jnp.zeros((16, 128), F32)
    for j in range(2):
        perm = jnp.where(dst == place + 64 * j, 1.0, 0.0).astype(BF)
        pick = jnp.where(row == (to % 8 * 2 + to // 8) * 2 + j, 1.0, 0.0).astype(BF)
        lanes = jnp.dot(out, perm, preferred_element_type=F32).astype(BF)
        acc = acc + jnp.dot(pick, lanes, preferred_element_type=F32)
    upper_ref[...] = acc[:8].astype(BF)
    lower_ref[...] = acc[8:].astype(BF)


def finish(blk, head, parts, const):
    vmem = pl.BlockSpec(memory_space=pltpu.VMEM)
    return pl.pallas_call(
        finish_body,
        in_specs=[pl.BlockSpec(memory_space=pltpu.SMEM)] * 2 + [vmem] * 5,
        out_shape=[jax.ShapeDtypeStruct((8, 128), BF)] * 2,
        compiler_params=pltpu.CompilerParams(vmem_limit_bytes=2 * MIB),
        name="finish",
    )(blk, head, *parts, const)


def spread_body(*refs):
    o_ref = refs[-1]
    rows = jnp.concatenate([ref[...].astype(F32) for ref in refs[:-1]], axis=0).astype(BF)
    o_ref[...] = jnp.broadcast_to(rows[None], o_ref.shape)


def spread(*rows):
    return ones_call(spread_body, jax.ShapeDtypeStruct((N, 32, 128), BF), 2, "spread")(*rows)


def conv_body(blk_ref, head_ref, r_ref, k1_ref, b1_ref, k2_ref, b2_ref, o_ref, win, feat, w1, w2):
    blank = jnp.zeros((16, CH), BF)
    for a in range(3):
        for wr in range(4):
            for wc in range(4):
                ry, p = divmod(wr, 2)
                row = ((a * 2 + ry) * 4 + wc) * 32 + p * 16
                for ey in range(2):
                    for ex in range(2):
                        b, g = wr - ey, wc - ex
                        hit = 0 <= b < 3 and 0 <= g < 3
                        tile = k1_ref[(a * 3 + b) * 3 + g] if hit else blank
                        w1[pl.ds(row, 16), pl.ds((ey * 2 + ex) * CH, CH)] = tile
    taps = ((1, 0, None, 2), (2, 1, 0, None))
    blank = jnp.zeros((32, CH), BF)
    for a in range(3):
        for u, pair in enumerate(((2, None), (1, 2), (0, 1), (None, 0))):
            for ey, b in enumerate(pair):
                for qi in range(2):
                    for n, g in enumerate(taps[qi]):
                        hit = b is not None and g is not None
                        tile = k2_ref[(a * 3 + b) * 3 + g] if hit else blank
                        span = pl.ds((ey * 2 + qi) * CH, CH)
                        w2[a, pl.ds(u * 128 + n * 32, 32), span] = tile

    rows = r_ref[...].astype(F32).reshape(512, 128)
    lane = lax.broadcasted_iota(jnp.int32, (512, 128), 1)
    col = lax.broadcasted_iota(jnp.int32, (512, 128), 0) % 16
    before = jnp.where(col == 0, 0.0, pltpu.roll(rows, 1, 0))
    after = jnp.where(col == 15, 0.0, pltpu.roll(rows, 511, 0))
    views = (
        pltpu.roll(jnp.where(lane < 96, rows, before), 32, 1),
        pltpu.roll(jnp.where(lane < 32, after, rows), 96, 1),
    )
    for j, view in enumerate(views):
        view = view.astype(BF).reshape(4, 8, 16, 128)
        for r in range(3):
            for ry in range(2):
                span = pl.ds(ry * 128, 128)
                win[j, 2:, r, :, span] = view[r + ry]
                for early in range(2):
                    win[j, early, r, :, span] = view[r + ry, 0]

    top = jnp.where(blk_ref[0] == 0, 0.0, 1.0)
    bottom = jnp.where(blk_ref[0] == N - 1, 0.0, 1.0)
    for j in range(2):
        lhs = jnp.concatenate([win[j, a : a + 8] for a in range(3)], axis=-1)
        lhs = lhs.reshape(8 * 3 * 16, lhs.shape[-1])
        for n in range(4):
            span = pl.ds(n * CH, CH)
            v = jnp.dot(lhs, w1[:, span], preferred_element_type=F32) + b1_ref[...]
            v = (v / (1.0 + jnp.exp(-v))).reshape(8, 3, 16, CH)
            for r in range(3):
                f = v[:, r]
                if (r, n // 2) == (0, 0):
                    f = f * top
                if (r, n // 2) == (2, 1):
                    f = f * bottom
                f = f.astype(BF)
                feat[j, 2:, r, :, span] = f
                feat[j, 0, r, :, span] = f[0]
                feat[j, 1, r, :, span] = f[0]

    def product(a, r, first):
        lhs = feat[:, a : a + 8, r].reshape(256, 4 * CH)
        rhs = w2[a, pl.ds(first, 256), :]
        return lax.dot_general(lhs, rhs, (((1,), (1,)), ((), ())), preferred_element_type=F32)

    src = lax.broadcasted_iota(jnp.int32, (CH, 128), 0)
    dst = lax.broadcasted_iota(jnp.int32, (CH, 128), 1) % 32 + head_ref[0] * 32
    pick = jnp.where(src == dst, 1.0, 0.0).astype(BF)
    terms = jnp.concatenate(bf16_terms(b2_ref[...]) + [jnp.zeros((5, CH), F32)], axis=0)
    terms = jnp.dot(terms.astype(BF), pick, preferred_element_type=F32)
    bias = terms[0:1] + terms[1:2] + terms[2:3]

    lane = lax.broadcasted_iota(jnp.int32, (128, 128), 1)
    col = lax.broadcasted_iota(jnp.int32, (128, 128), 0) % 16
    for pair in range(2):
        acc = jnp.zeros((256, 256), F32)
        for a in range(3):
            acc = acc + product(a, pair, 256) + product(a, pair + 1, 0)
        for y in range(2):
            z = acc[:, y * 128 : (y + 1) * 128]
            z0, z1 = z[:128], z[128:]
            right = jnp.where(col == 0, 0.0, pltpu.roll(z1, 1, 0))
            left = jnp.where(col == 15, 0.0, pltpu.roll(z0, 127, 0))
            s0 = z0 + pltpu.roll(jnp.where(lane < 96, right, z1), 64, 1)
            s1 = z1 + pltpu.roll(jnp.where(lane < 96, z0, left), 64, 1)
            out = jnp.where(lane < 64, s0, pltpu.roll(s1, 64, 1)) + bias
            o_ref[pair * 2 + y] = out.astype(BF).reshape(8, 16, 128)


def conv_stage(blk, head, rows, k1, b1, k2, b2):
    vmem = pl.BlockSpec(memory_space=pltpu.VMEM)
    return pl.pallas_call(
        conv_body,
        in_specs=[pl.BlockSpec(memory_space=pltpu.SMEM)] * 2 + [vmem] * 5,
        out_shape=jax.ShapeDtypeStruct((4, 8, 16, 128), BF),
        scratch_shapes=[
            pltpu.VMEM((2, 10, 3, 16, 256), BF),
            pltpu.VMEM((2, 10, 3, 16, 4 * CH), BF),
            pltpu.VMEM((768, 4 * CH), BF),
            pltpu.VMEM((3, 512, 4 * CH), BF),
        ],
        compiler_params=pltpu.CompilerParams(vmem_limit_bytes=24 * MIB),
        name="convs",
    )(blk, head, rows, k1, b1, k2, b2)


def after(value, *others):
    return lax.optimization_barrier((value,) + others)[0]


def shards(
    qkv,
    query_blocks,
    out_weight,
    mod_shift,
    mod_scale,
    final_weight,
    final_bias,
    conv_in_weight,
    conv_in_bias,
    conv_weight,
    conv_bias,
):
    head = lax.axis_index("head")
    blk = lax.axis_index("blk")
    core = blk % 2
    side = head % 2
    blk_at, head_at = blk.reshape(1), head.reshape(1)

    q_send = split_heads(qkv, (0,))
    quarter = D // 4
    mine, theirs = (side * 2 + core) * quarter, ((1 - side) * 2 + core) * quarter
    source = after(out_weight, q_send)
    part = lax.dynamic_slice_in_dim(source, mine, quarter, axis=1)
    given = lax.dynamic_slice_in_dim(source, theirs, quarter, axis=1)
    pair = jnp.stack([part, lax.ppermute(given, "head", NEXT_SWAP)])

    q_all = lax.all_to_all(q_send, "head", 0, 0, tiled=True)
    kv_send = after(split_heads(qkv, (1, 2)), q_all, pair)
    kv_got = lax.all_to_all(kv_send, "head", 0, 0, tiled=True).reshape(-1, 2 * HD)
    weight_a = lax.all_gather(
        after(pair, kv_got), "head", axis=0, tiled=True, axis_index_groups=GROUPS_Z
    )

    near = select_queries(query_blocks, q_all)
    both = jnp.concatenate([near, lax.ppermute(near, "blk", FAR_SWAP)], axis=0)
    queries = [both]
    for m in range(1, 4):
        queries.append(lax.ppermute(both, "blk", Y_SWAPS[m]))
    kv_own = after(kv_got, *queries)
    kv_other = lax.ppermute(kv_own, "blk", NEXT_SWAP)

    keys, vals = pack(kv_own, kv_other)
    part_1 = attention(queries[1], keys, vals)
    got_1 = lax.ppermute(part_1, "blk", Y_SWAPS[1])
    part_2 = attention(after(queries[2], part_1), keys, vals)
    got_2 = lax.ppermute(part_2, "blk", Y_SWAPS[2])
    part_3 = attention(after(queries[3], part_2, got_1), keys, vals)
    got_3 = lax.ppermute(part_3, "blk", Y_SWAPS[3])
    part_0 = attention(after(queries[0], part_3, got_2), keys, vals)
    parts = (part_0, got_1, got_2, got_3)
    far_rows = lax.ppermute(merge(1, parts), "blk", FAR_SWAP)

    attended = merge_last(merge(0, parts), far_rows)
    attended = lax.all_to_all(attended, "head", 0, 0, tiled=True)
    other = lax.ppermute(attended, "blk", NEXT_SWAP)
    weight = after(weight_a, attended).reshape(HEADS * HD, quarter)
    own, to_side, to_core, to_both, const = project(
        blk_at,
        head_at,
        attended,
        other,
        weight,
        mod_scale.reshape(1, D),
        mod_shift.reshape(1, D),
        jnp.transpose(final_weight),
        final_bias.reshape(1, 64),
    )
    shares = (
        own,
        lax.ppermute(to_side, "head", NEXT_SWAP),
        lax.ppermute(to_core, "blk", NEXT_SWAP),
        lax.ppermute(to_both, ("head", "blk"), BOTH_SWAP),
    )
    upper, lower = finish(blk_at, head_at, shares, const)

    ends = N - 1
    above = lax.ppermute(lower, "blk", [(i, i + 1) for i in range(ends)])
    below = lax.ppermute(upper, "blk", [(i + 1, i) for i in range(ends)])
    rows = lax.all_to_all(spread(above, upper, lower, below), "head", 0, 0, tiled=True)
    out = conv_stage(
        blk_at,
        head_at,
        jnp.transpose(rows, (1, 0, 2)),
        conv_in_weight.reshape(27, 16, CH),
        conv_in_bias.reshape(1, CH),
        jnp.transpose(conv_weight, (0, 1, 2, 4, 3)).reshape(27, 32, CH),
        conv_bias.reshape(1, CH),
    )
    out = lax.all_to_all(jnp.transpose(out, (2, 0, 1, 3)), "head", 0, 0, tiled=True)
    out = jnp.transpose(out.reshape(N, 4, 8, 4, 32), (2, 1, 3, 0, 4))
    return out.reshape(8, 4, 4, CH)


def solution(mesh):
    in_specs = (
        P("blk", "head", None),
        P("blk"),
        P("head", None),
        P(),
        P(),
        P(),
        P(),
        P(),
        P(),
        P(None, None, None, None, "head"),
        P(),
    )
    out_specs = P(None, "blk", "head", None)
    return jax.shard_map(shards, mesh=mesh, in_specs=in_specs, out_specs=out_specs, check_vma=False)
```

```python
import functools
import math

import jax
import jax.numpy as jnp
from jax import lax
from jax.experimental import pallas as pl
from jax.experimental.pallas import tpu as pltpu
from jax.sharding import PartitionSpec as P

HEADS = 16
HD = 128
D = 3072
QBLK = 128
QROWS = 512
CH = 512
NORM_EPS = 1e-06
BF = jnp.bfloat16
F32 = jnp.float32
COEF = math.log2(math.e) / math.sqrt(HD)
MIB = 2**20

N = 16
GROUPS_Z = [[x + 2 * k for k in range(8)] for x in range(2)]
NEXT_SWAP = [(i, i ^ 1) for i in range(N)]
Y_SWAPS = [[(i, i ^ (2 * m)) for i in range(N)] for m in range(4)]
BOTH_SWAP = [(h * N + b, (h ^ 1) * N + (b ^ 1)) for h in range(N) for b in range(N)]
FAR_SWAP = [(i, i ^ 8) for i in range(N)]


def ones_call(body, out_shape, limit, name):
    return pl.pallas_call(
        body,
        out_shape=out_shape,
        compiler_params=pltpu.CompilerParams(vmem_limit_bytes=limit * MIB),
        name=name,
    )


def split_body(*refs):
    o_ref = refs[-1]
    for n, ref in enumerate(refs[:-1]):
        for h in range(HEADS):
            o_ref[h, :, n * HD : (n + 1) * HD] = ref[0, :, h * HD : (h + 1) * HD]


def split_heads(qkv, parts):
    tok = qkv.shape[1]
    return pl.pallas_call(
        split_body,
        grid=(1,),
        in_specs=[
            pl.BlockSpec((1, tok, HEADS * HD), lambda i, p=p: (0, 0, p)) for p in parts
        ],
        out_specs=pl.BlockSpec((HEADS, tok, len(parts) * HD), lambda i: (0, 0, 0)),
        out_shape=jax.ShapeDtypeStruct((HEADS, tok, len(parts) * HD), BF),
        compiler_params=pltpu.CompilerParams(vmem_limit_bytes=56 * MIB),
        name="split",
    )(*[qkv] * len(parts))


def select_body(chosen_ref, q_ref, o_ref):
    for i in range(QROWS // QBLK):
        o_ref[pl.ds(i * QBLK, QBLK), :] = q_ref[chosen_ref[i] % N]


def select_queries(chosen, q_all):
    return pl.pallas_call(
        select_body,
        in_specs=[
            pl.BlockSpec(memory_space=pltpu.SMEM),
            pl.BlockSpec(memory_space=pltpu.VMEM),
        ],
        out_shape=jax.ShapeDtypeStruct((QROWS, HD), BF),
        compiler_params=pltpu.CompilerParams(vmem_limit_bytes=4 * MIB),
        name="select",
    )(chosen, q_all)


def pack_body(own_ref, other_ref, keys, vals):
    half = own_ref.shape[0]
    for s, ref in enumerate((own_ref, other_ref)):
        rows = pl.ds(s * half, half)
        keys[rows, :HD] = ref[:, :HD]
        keys[rows, HD:] = ref[:, :HD]
        vals[rows, :HD] = ref[:, HD:]
        vals[rows, HD:] = jnp.ones((half, HD), BF)


def pack(own, other):
    shape = jax.ShapeDtypeStruct((2 * own.shape[0], 2 * HD), BF)
    return ones_call(pack_body, [shape, shape], 8, "pack")(own, other)


def store_lse(o_ref, chunk, lse):
    hi = lse.astype(BF).astype(F32)
    mid = (lse - hi).astype(BF).astype(F32)
    low = lse - hi - mid
    tail = jnp.concatenate([hi, mid, low, jnp.zeros_like(hi)], axis=0)
    o_ref[chunk, QROWS:, :] = tail.astype(BF)


def load_lse(ref, s):
    tail = ref[s, QROWS:, :].astype(F32)
    return tail[0:4] + tail[4:8] + tail[8:12]


def column(row):
    return jnp.transpose(jnp.broadcast_to(row, (128, 128)))


def attention_body(sub, q_ref, keys, vals, o_ref):
    def scores(chunk, first):
        q = q_ref[pl.ds(chunk * QROWS + first, sub), :].astype(F32) * COEF
        hi = q.astype(BF)
        lo = (q - hi.astype(F32)).astype(BF)
        return lax.dot_general(
            jnp.concatenate([hi, lo], axis=1),
            keys[...],
            (((1,), (1,)), ((), ())),
            preferred_element_type=F32,
        )

    tiles = [(chunk, first) for chunk in range(2) for first in range(0, QROWS, sub)]
    lse_rows = []
    current = scores(*tiles[0])
    for n, (chunk, first) in enumerate(tiles):
        later = scores(*tiles[n + 1]) if n + 1 < len(tiles) else None
        high = jnp.max(current, axis=1, keepdims=True)
        weights = jnp.exp2(current - high).astype(BF)
        acc = jnp.dot(weights, vals[...], preferred_element_type=F32)
        total = acc[:, HD:]
        o_ref[chunk, first : first + sub, :] = (acc[:, :HD] / total).astype(BF)
        lse = high + jnp.log2(total)
        for k in range(sub // 128):
            lse_rows.append(jnp.transpose(lse[k * 128 : (k + 1) * 128])[:1])
        if first + sub == QROWS:
            store_lse(o_ref, chunk, jnp.concatenate(lse_rows, axis=0))
            lse_rows = []
        current = later


def attention(queries, keys, vals):
    count = keys.shape[0]
    return pl.pallas_call(
        functools.partial(attention_body, QROWS),
        in_specs=[pl.BlockSpec(memory_space=pltpu.VMEM)] * 3,
        out_shape=jax.ShapeDtypeStruct((2, QROWS + 16, HD), BF),
        compiler_params=pltpu.CompilerParams(vmem_limit_bytes=40 * MIB),
        cost_estimate=pl.CostEstimate(
            flops=12 * 2 * QROWS * count * 2 * HD,
            bytes_accessed=4 * MIB,
            transcendentals=2 * QROWS * count,
        ),
        name="attention",
    )(queries, keys, vals)


def merged(refs, n):
    lses = [load_lse(ref, n) for ref in refs]
    high = functools.reduce(jnp.maximum, lses)
    shares = [jnp.exp2(v - high) for v in lses]
    total = functools.reduce(jnp.add, shares)
    shares = [v / total for v in shares]
    blocks = []
    for k in range(4):
        acc = jnp.zeros((128, HD), F32)
        for share, ref in zip(shares, refs):
            part = ref[n, pl.ds(k * 128, 128), :].astype(F32)
            acc = acc + column(share[k : k + 1]) * part
        blocks.append(acc.astype(BF))
    return blocks, high + jnp.log2(total)


def merge_body(n, *refs):
    o_ref = refs[-1]
    blocks, lse = merged(refs[:-1], n)
    for k, block in enumerate(blocks):
        o_ref[0, pl.ds(k * 128, 128), :] = block
    store_lse(o_ref, 0, lse)


def merge(n, parts):
    shape = jax.ShapeDtypeStruct((1, QROWS + 16, HD), BF)
    return ones_call(functools.partial(merge_body, n), shape, 8, "merge")(*parts)


def merge_last_body(a_ref, b_ref, o_ref):
    blocks, _ = merged((a_ref, b_ref), 0)
    for k, block in enumerate(blocks):
        for n in range(4):
            o_ref[k * 4 + n] = block[n // 2 * 64 : n // 2 * 64 + 64]


def merge_last(a, b):
    shape = jax.ShapeDtypeStruct((N, 64, HD), BF)
    return ones_call(merge_last_body, shape, 8, "merge_last")(a, b)


def bf16_terms(v):
    hi = v.astype(BF).astype(F32)
    mid = (v - hi).astype(BF).astype(F32)
    return [hi, mid, v - hi - mid]


def project_body(
    blk_ref, head_ref, att_ref, other_ref, w_ref, scale_ref, shift_ref, fw_ref, fb_ref, *refs
):
    own_ref, side_ref, core_ref, both_ref, const_ref, rows, stats = refs
    core, side = blk_ref[0] % 2, head_ref[0] % 2
    count, cols = att_ref.shape[1], w_ref.shape[1]
    contract = (((1,), (1,)), ((), ()))
    for h in range(HEADS):
        rows[:count, h * HD : (h + 1) * HD] = att_ref[h ^ side]
        rows[count:, h * HD : (h + 1) * HD] = other_ref[h ^ side]
    x = jnp.dot(rows[...], w_ref[...], preferred_element_type=F32)

    moved = jnp.zeros((1, 128), F32)
    blank = jnp.zeros((64, cols), BF)
    for s in range(4):
        span = pl.ds(s * cols, cols)
        terms = bf16_terms(1.0 + scale_ref[:, span]) + bf16_terms(shift_ref[:, span])
        lhs = jnp.concatenate(terms + [jnp.zeros((2, cols), F32)], axis=0).astype(BF)
        rhs = jnp.concatenate([fw_ref[:, span], blank], axis=0)
        got = lax.dot_general(lhs, rhs, contract, preferred_element_type=F32)
        const_ref[s : s + 1, :] = got[0:1] + got[1:2] + got[2:3]
        moved = moved + got[3:4] + got[4:5] + got[5:6]
    const_ref[4:5, :] = moved
    const_ref[4:5, :64] = moved[:, :64] + fb_ref[...]

    mean = jnp.sum(x, axis=1, keepdims=True) * (1.0 / cols)
    x = x - mean
    square = jnp.sum(x * x, axis=1, keepdims=True)
    span = pl.ds(pl.multiple_of((side * 2 + core) * cols, 128), cols)
    m = (x * (1.0 + scale_ref[:, span])).astype(BF)
    rhs = jnp.concatenate([fw_ref[:, span], blank], axis=0)
    acc = lax.dot_general(m, rhs, contract, preferred_element_type=F32)
    lane = lax.broadcasted_iota(jnp.int32, stats.shape, 1)
    stats[...] = jnp.where(lane < 64, acc, jnp.where(lane < 96, mean, square))
    mine, theirs = pl.multiple_of(side * 32, 32), pl.multiple_of(32 - side * 32, 32)
    own_ref[...] = stats[pl.ds(mine, 32), :]
    side_ref[...] = stats[pl.ds(theirs, 32), :]
    core_ref[...] = stats[pl.ds(count + mine, 32), :]
    both_ref[...] = stats[pl.ds(count + theirs, 32), :]


def project(blk, head, att, other, w, scale, shift, fw, fb):
    count = att.shape[1]
    vmem = pl.BlockSpec(memory_space=pltpu.VMEM)
    outs = [(32, 128)] * 4 + [(8, 128)]
    return pl.pallas_call(
        project_body,
        in_specs=[pl.BlockSpec(memory_space=pltpu.SMEM)] * 2 + [vmem] * 7,
        out_shape=[jax.ShapeDtypeStruct(o, F32) for o in outs],
        scratch_shapes=[
            pltpu.VMEM((2 * count, HEADS * HD), BF),
            pltpu.VMEM((2 * count, 128), F32),
        ],
        compiler_params=pltpu.CompilerParams(vmem_limit_bytes=12 * MIB),
        name="project",
    )(blk, head, att, other, w, scale, shift, fw, fb)


def finish_body(blk_ref, head_ref, *refs):
    const_ref, upper_ref, lower_ref = refs[4:]
    core, side = blk_ref[0] % 2, head_ref[0] % 2
    parts = [ref[...] for ref in refs[:4]]
    places = [(side, core), (1 - side, core), (side, 1 - core), (1 - side, 1 - core)]
    means = [part[:, 64:65] for part in parts]
    mean = sum(means) * 0.25
    total = sum(parts)
    square = total[:, 96:97]
    for (s, c), own in zip(places, means):
        apart = own - mean
        square = square + apart * apart * (D / 4)
        total = total + apart * const_ref[pl.ds(s * 2 + c, 1), :]
    rstd = lax.rsqrt(square * (1.0 / D) + NORM_EPS)
    out = (total * rstd + const_ref[4:5, :]).astype(BF)[:, :64]

    src = lax.broadcasted_iota(jnp.int32, (64, 128), 0)
    dst = lax.broadcasted_iota(jnp.int32, (64, 128), 1)
    place = (src % 2) * 32 + (src // 2 % 2) * 16 + src // 4
    to = lax.broadcasted_iota(jnp.int32, (16, 32), 0)
    row = lax.broadcasted_iota(jnp.int32, (16, 32), 1)
    acc = jnp.zeros((16, 128), F32)
    for j in range(2):
        perm = jnp.where(dst == place + 64 * j, 1.0, 0.0).astype(BF)
        pick = jnp.where(row == (to % 8 * 2 + to // 8) * 2 + j, 1.0, 0.0).astype(BF)
        lanes = jnp.dot(out, perm, preferred_element_type=F32).astype(BF)
        acc = acc + jnp.dot(pick, lanes, preferred_element_type=F32)
    upper_ref[...] = acc[:8].astype(BF)
    lower_ref[...] = acc[8:].astype(BF)


def finish(blk, head, parts, const):
    vmem = pl.BlockSpec(memory_space=pltpu.VMEM)
    return pl.pallas_call(
        finish_body,
        in_specs=[pl.BlockSpec(memory_space=pltpu.SMEM)] * 2 + [vmem] * 5,
        out_shape=[jax.ShapeDtypeStruct((8, 128), BF)] * 2,
        compiler_params=pltpu.CompilerParams(vmem_limit_bytes=2 * MIB),
        name="finish",
    )(blk, head, *parts, const)


def spread_body(*refs):
    o_ref = refs[-1]
    rows = jnp.concatenate([ref[...].astype(F32) for ref in refs[:-1]], axis=0).astype(BF)
    o_ref[...] = jnp.broadcast_to(rows[None], o_ref.shape)


def spread(*rows):
    return ones_call(spread_body, jax.ShapeDtypeStruct((N, 32, 128), BF), 2, "spread")(*rows)


def conv_body(blk_ref, head_ref, r_ref, k1_ref, b1_ref, k2_ref, b2_ref, o_ref, win, feat, w1, w2):
    blank = jnp.zeros((16, CH), BF)
    for a in range(3):
        for wr in range(4):
            for wc in range(4):
                ry, p = divmod(wr, 2)
                row = ((a * 2 + ry) * 4 + wc) * 32 + p * 16
                for ey in range(2):
                    for ex in range(2):
                        b, g = wr - ey, wc - ex
                        hit = 0 <= b < 3 and 0 <= g < 3
                        tile = k1_ref[(a * 3 + b) * 3 + g] if hit else blank
                        w1[pl.ds(row, 16), pl.ds((ey * 2 + ex) * CH, CH)] = tile
    taps = ((1, 0, None, 2), (2, 1, 0, None))
    blank = jnp.zeros((32, CH), BF)
    for a in range(3):
        for u, pair in enumerate(((2, None), (1, 2), (0, 1), (None, 0))):
            for ey, b in enumerate(pair):
                for qi in range(2):
                    for n, g in enumerate(taps[qi]):
                        hit = b is not None and g is not None
                        tile = k2_ref[(a * 3 + b) * 3 + g] if hit else blank
                        span = pl.ds((ey * 2 + qi) * CH, CH)
                        w2[a, pl.ds(u * 128 + n * 32, 32), span] = tile

    rows = r_ref[...].astype(F32).reshape(512, 128)
    lane = lax.broadcasted_iota(jnp.int32, (512, 128), 1)
    col = lax.broadcasted_iota(jnp.int32, (512, 128), 0) % 16
    before = jnp.where(col == 0, 0.0, pltpu.roll(rows, 1, 0))
    after = jnp.where(col == 15, 0.0, pltpu.roll(rows, 511, 0))
    views = (
        pltpu.roll(jnp.where(lane < 96, rows, before), 32, 1),
        pltpu.roll(jnp.where(lane < 32, after, rows), 96, 1),
    )
    for j, view in enumerate(views):
        view = view.astype(BF).reshape(4, 8, 16, 128)
        for r in range(3):
            for ry in range(2):
                span = pl.ds(ry * 128, 128)
                win[j, 2:, r, :, span] = view[r + ry]
                for early in range(2):
                    win[j, early, r, :, span] = view[r + ry, 0]

    top = jnp.where(blk_ref[0] == 0, 0.0, 1.0)
    bottom = jnp.where(blk_ref[0] == N - 1, 0.0, 1.0)
    for j in range(2):
        lhs = jnp.concatenate([win[j, a : a + 8] for a in range(3)], axis=-1)
        lhs = lhs.reshape(8 * 3 * 16, lhs.shape[-1])
        for n in range(4):
            span = pl.ds(n * CH, CH)
            v = jnp.dot(lhs, w1[:, span], preferred_element_type=F32) + b1_ref[...]
            v = (v / (1.0 + jnp.exp(-v))).reshape(8, 3, 16, CH)
            for r in range(3):
                f = v[:, r]
                if (r, n // 2) == (0, 0):
                    f = f * top
                if (r, n // 2) == (2, 1):
                    f = f * bottom
                f = f.astype(BF)
                feat[j, 2:, r, :, span] = f
                feat[j, 0, r, :, span] = f[0]
                feat[j, 1, r, :, span] = f[0]

    def product(a, r, first):
        lhs = feat[:, a : a + 8, r].reshape(256, 4 * CH)
        rhs = w2[a, pl.ds(first, 256), :]
        return lax.dot_general(lhs, rhs, (((1,), (1,)), ((), ())), preferred_element_type=F32)

    src = lax.broadcasted_iota(jnp.int32, (CH, 128), 0)
    dst = lax.broadcasted_iota(jnp.int32, (CH, 128), 1) % 32 + head_ref[0] * 32
    pick = jnp.where(src == dst, 1.0, 0.0).astype(BF)
    terms = jnp.concatenate(bf16_terms(b2_ref[...]) + [jnp.zeros((5, CH), F32)], axis=0)
    terms = jnp.dot(terms.astype(BF), pick, preferred_element_type=F32)
    bias = terms[0:1] + terms[1:2] + terms[2:3]

    lane = lax.broadcasted_iota(jnp.int32, (128, 128), 1)
    col = lax.broadcasted_iota(jnp.int32, (128, 128), 0) % 16
    for pair in range(2):
        acc = jnp.zeros((256, 256), F32)
        for a in range(3):
            acc = acc + product(a, pair, 256) + product(a, pair + 1, 0)
        for y in range(2):
            z = acc[:, y * 128 : (y + 1) * 128]
            z0, z1 = z[:128], z[128:]
            right = jnp.where(col == 0, 0.0, pltpu.roll(z1, 1, 0))
            left = jnp.where(col == 15, 0.0, pltpu.roll(z0, 127, 0))
            s0 = z0 + pltpu.roll(jnp.where(lane < 96, right, z1), 64, 1)
            s1 = z1 + pltpu.roll(jnp.where(lane < 96, z0, left), 64, 1)
            out = jnp.where(lane < 64, s0, pltpu.roll(s1, 64, 1)) + bias
            o_ref[pair * 2 + y] = out.astype(BF).reshape(8, 16, 128)


def conv_stage(blk, head, rows, k1, b1, k2, b2):
    vmem = pl.BlockSpec(memory_space=pltpu.VMEM)
    return pl.pallas_call(
        conv_body,
        in_specs=[pl.BlockSpec(memory_space=pltpu.SMEM)] * 2 + [vmem] * 5,
        out_shape=jax.ShapeDtypeStruct((4, 8, 16, 128), BF),
        scratch_shapes=[
            pltpu.VMEM((2, 10, 3, 16, 256), BF),
            pltpu.VMEM((2, 10, 3, 16, 4 * CH), BF),
            pltpu.VMEM((768, 4 * CH), BF),
            pltpu.VMEM((3, 512, 4 * CH), BF),
        ],
        compiler_params=pltpu.CompilerParams(vmem_limit_bytes=24 * MIB),
        name="convs",
    )(blk, head, rows, k1, b1, k2, b2)


def after(value, *others):
    return lax.optimization_barrier((value,) + others)[0]


def shards(
    qkv,
    query_blocks,
    out_weight,
    mod_shift,
    mod_scale,
    final_weight,
    final_bias,
    conv_in_weight,
    conv_in_bias,
    conv_weight,
    conv_bias,
):
    head = lax.axis_index("head")
    blk = lax.axis_index("blk")
    core = blk % 2
    side = head % 2
    blk_at, head_at = blk.reshape(1), head.reshape(1)

    q_send = split_heads(qkv, (0,))
    quarter = D // 4
    mine, theirs = (side * 2 + core) * quarter, ((1 - side) * 2 + core) * quarter
    source = after(out_weight, q_send)
    part = lax.dynamic_slice_in_dim(source, mine, quarter, axis=1)
    given = lax.dynamic_slice_in_dim(source, theirs, quarter, axis=1)
    pair = jnp.stack([part, lax.ppermute(given, "head", NEXT_SWAP)])

    q_all = lax.all_to_all(q_send, "head", 0, 0, tiled=True)
    kv_send = after(split_heads(qkv, (1, 2)), q_all, pair)
    kv_got = lax.all_to_all(kv_send, "head", 0, 0, tiled=True).reshape(-1, 2 * HD)
    weight_a = lax.all_gather(
        after(pair, kv_got), "head", axis=0, tiled=True, axis_index_groups=GROUPS_Z
    )

    near = select_queries(query_blocks, q_all)
    both = jnp.concatenate([near, lax.ppermute(near, "blk", FAR_SWAP)], axis=0)
    queries = [both]
    for m in range(1, 4):
        queries.append(lax.ppermute(both, "blk", Y_SWAPS[m]))
    kv_own = after(kv_got, *queries)
    kv_other = lax.ppermute(kv_own, "blk", NEXT_SWAP)

    keys, vals = pack(kv_own, kv_other)
    part_1 = attention(queries[1], keys, vals)
    got_1 = lax.ppermute(part_1, "blk", Y_SWAPS[1])
    part_2 = attention(after(queries[2], part_1), keys, vals)
    got_2 = lax.ppermute(part_2, "blk", Y_SWAPS[2])
    part_3 = attention(after(queries[3], part_2, got_1), keys, vals)
    got_3 = lax.ppermute(part_3, "blk", Y_SWAPS[3])
    part_0 = attention(after(queries[0], part_3, got_2), keys, vals)
    parts = (part_0, got_1, got_2, got_3)
    far_rows = lax.ppermute(merge(1, parts), "blk", FAR_SWAP)

    attended = merge_last(merge(0, parts), far_rows)
    attended = lax.all_to_all(attended, "head", 0, 0, tiled=True)
    other = lax.ppermute(attended, "blk", NEXT_SWAP)
    weight = after(weight_a, attended).reshape(HEADS * HD, quarter)
    own, to_side, to_core, to_both, const = project(
        blk_at,
        head_at,
        attended,
        other,
        weight,
        mod_scale.reshape(1, D),
        mod_shift.reshape(1, D),
        jnp.transpose(final_weight),
        final_bias.reshape(1, 64),
    )
    shares = (
        own,
        lax.ppermute(to_side, "head", NEXT_SWAP),
        lax.ppermute(to_core, "blk", NEXT_SWAP),
        lax.ppermute(to_both, ("head", "blk"), BOTH_SWAP),
    )
    upper, lower = finish(blk_at, head_at, shares, const)

    ends = N - 1
    above = lax.ppermute(lower, "blk", [(i, i + 1) for i in range(ends)])
    below = lax.ppermute(upper, "blk", [(i + 1, i) for i in range(ends)])
    rows = lax.all_to_all(spread(above, upper, lower, below), "head", 0, 0, tiled=True)
    out = conv_stage(
        blk_at,
        head_at,
        jnp.transpose(rows, (1, 0, 2)),
        conv_in_weight.reshape(27, 16, CH),
        conv_in_bias.reshape(1, CH),
        jnp.transpose(conv_weight, (0, 1, 2, 4, 3)).reshape(27, 32, CH),
        conv_bias.reshape(1, CH),
    )
    out = lax.all_to_all(jnp.transpose(out, (2, 0, 1, 3)), "head", 0, 0, tiled=True)
    out = jnp.transpose(out.reshape(N, 4, 8, 4, 32), (2, 1, 3, 0, 4))
    return out.reshape(8, 4, 4, CH)


def solution(mesh):
    in_specs = (
        P("blk", "head", None),
        P("blk"),
        P("head", None),
        P(),
        P(),
        P(),
        P(),
        P(),
        P(),
        P(None, None, None, None, "head"),
        P(),
    )
    out_specs = P(None, "blk", "head", None)
    return jax.shard_map(shards, mesh=mesh, in_specs=in_specs, out_specs=out_specs, check_vma=False)
```
